32 devices in a mesh: face: 8 (over y, x, core), tile: 4 (over z).
Axes of the slice: x: 2, y: 2, z: 4, core: 2. Of those that a mesh axis runs over, the one named last changes fastest.
Arguments:
- state: float32 [32, 4, 2, 128, 128], P(('face', 'tile')), may hold values from -3 to 3
- forcing: float32 [32, 2, 4, 128, 128], P(('face', 'tile')), may hold values from -3 to 3
- cotangent: float32 [32, 4, 2, 128, 128], P(('face', 'tile')), may hold values from -6 to 6
- neighbour: int32 [32, 4], P(('face', 'tile')), may hold values from -1 to 31, as said below
- rotation: int32 [32, 4], P(('face', 'tile')), may hold values from 0 to 7
- wet: int32 [32], P(('face', 'tile')), may hold values from 0 to 1, as said below
- levels: int32 [32, 128, 128], P(('face', 'tile')), may hold values from 0 to 2
Outputs:
- state_gradient: float32 [32, 4, 2, 128, 128], P(('face', 'tile'))
- forcing_gradient: float32 [32, 2, 4, 128, 128], P(('face', 'tile'))
The draws below stay inside these ranges and needn't reach their ends.
Inputs may be any that keep to these rules, and one draw needn't show every extreme that they name: The west neighbour of every tile is the tile of the same slot on the device with the same tile index at face index one below (wrapping around the face axis), the east neighbour the one at face index one above; south and north neighbours lie on a device of the same face block or are -1. Every tile on a device of tile index 0 is wet.
All inputs are finite; a program needn't handle non-finite values.
Results may differ from the reference program's by a relative error of at most 0.00005.
Values sent between devices are 32-bit elements; how exact they have to be, the bound alone decides.
A program may use at most 64 MiB of HBM per device.

```python
import jax
import jax.numpy as jnp

FIELDS = 4
LEVELS = 2
TSIDE = 128
SLOTS = 1
STEPS = 2
FACE_ROWS = 8
GROUP = 4
NTILES = 32


def draw_neighbour(key, part):
    ids = jnp.arange(NTILES, dtype=jnp.int32)[:, None]
    device = ids // SLOTS
    own_slot = ids % SLOTS
    face_idx = device // GROUP
    tile_idx = device % GROUP
    key_kind, key_tile, key_slot = jax.random.split(key, 3)
    kind = jax.random.randint(key_kind, (NTILES, 4), 0, 5, dtype=jnp.int32)
    other_tile = jax.random.randint(key_tile, (NTILES, 4), 0, GROUP, dtype=jnp.int32)
    slot = jax.random.randint(key_slot, (NTILES, 4), 0, SLOTS, dtype=jnp.int32)
    lower = (face_idx + FACE_ROWS - 1) % FACE_ROWS
    upper = (face_idx + 1) % FACE_ROWS
    sides = jnp.arange(4, dtype=jnp.int32)[None, :]
    across_low = (lower * GROUP + tile_idx) * SLOTS + own_slot
    across_high = (upper * GROUP + tile_idx) * SLOTS + own_slot
    inside = (face_idx * GROUP + other_tile) * SLOTS + slot
    inside = jnp.where(kind == 0, -1, inside)
    result = jnp.where(sides == 0, across_low, jnp.where(sides == 1, across_high, inside))
    return result.astype(jnp.int32)


def draw_wet(key, part):
    ids = jnp.arange(NTILES, dtype=jnp.int32)
    tile_idx = ids // SLOTS % GROUP
    pick = jax.random.randint(key, (NTILES,), 0, 4, dtype=jnp.int32)
    return jnp.where((tile_idx == 0) | (pick < 3), 1, 0).astype(jnp.int32)


def set_ends(array, key, low, largest):
    longest = array.shape.index(max(array.shape))
    spots = []
    for shift in (0, 1):
        where = [jax.random.randint(jax.random.fold_in(key, axis), (), 0, length) for axis, length in enumerate(array.shape)]
        where[longest] = (where[longest] + shift) % array.shape[longest]
        spots.append(tuple(where))
    return array.at[spots[0]].set(low).at[spots[1]].set(largest)


def block_levels(key, extent, cuts, smallest, high):
    gain, own = 1.0, jax.random.fold_in(key, 6)
    for axis_at, parts in cuts:
        heights = jnp.exp(jax.random.uniform(jax.random.fold_in(own, axis_at), (parts,), jnp.float32, smallest / len(cuts), high / len(cuts)))
        gain = gain * jnp.repeat(heights, extent[axis_at] // parts).reshape([-1 if axis == axis_at else 1 for axis in range(len(extent))])
    return gain


def gaussian(own_key, extent, deviation, bound, cuts=(), held_as=jnp.bfloat16):
    loudness = block_levels(own_key, extent, cuts, -0.22, 0.18) if cuts else 1.0
    entries = jax.random.normal(own_key, extent, jnp.float32) * deviation * loudness
    return jnp.minimum(jnp.maximum(entries, -bound), bound).astype(held_as)


def setup_inputs(seed: int = 0) -> dict:
    keys = jax.random.split(jax.random.key(seed), 8)
    state = gaussian(keys[0], (NTILES, FIELDS, LEVELS, TSIDE, TSIDE), 0.5, 3.0, ((0, 32),), jnp.float32)
    forcing = gaussian(keys[1], (NTILES, STEPS, FIELDS, TSIDE, TSIDE), 0.5, 3.0, ((0, 32),), jnp.float32)
    cotangent = gaussian(keys[2], (NTILES, FIELDS, LEVELS, TSIDE, TSIDE), 1.0, 6.0, ((0, 32),), jnp.float32)
    neighbour = draw_neighbour(jax.random.fold_in(keys[7], 71), 0)
    rotation = set_ends(jax.random.randint(keys[4], (NTILES, 4), 0, 8), jax.random.fold_in(keys[4], 1), 0, 7).astype(jnp.int32)
    wet = draw_wet(jax.random.fold_in(keys[7], 71), 0)
    levels = set_ends(jax.random.randint(keys[6], (NTILES, TSIDE, TSIDE), 0, LEVELS + 1), jax.random.fold_in(keys[6], 1), 0, LEVELS).astype(jnp.int32)
    return dict(state=state, forcing=forcing, cotangent=cotangent, neighbour=neighbour, rotation=rotation, wet=wet, levels=levels)


time_step = 1.0
diffuse_rate = 0.15
viscosity = 0.15
vertical_mix = 0.1
coriolis = 0.3
buoyancy_scale = 0.25
thermal_coef = 1.0
haline_coef = 0.8
drag_rate = 0.05

def edge_strips(field):
    return jnp.stack([field[..., :, 0], field[..., :, -1], field[..., 0, :], field[..., -1, :]], axis=1)

def place_halo(field, halos):
    padded = jnp.pad(field, ((0, 0), (0, 0), (0, 0), (1, 1), (1, 1)))
    padded = padded.at[..., 1:-1, 0].set(halos[:, 0])
    padded = padded.at[..., 1:-1, -1].set(halos[:, 1])
    padded = padded.at[..., 0, 1:-1].set(halos[:, 2])
    padded = padded.at[..., -1, 1:-1].set(halos[:, 3])
    return padded

def level_mix(values):
    above = jnp.concatenate([values[:, :1], values[:, :-1]], axis=1)
    below = jnp.concatenate([values[:, 1:], values[:, -1:]], axis=1)
    return above + below - 2.0 * values

def step_tiles(padded, mask, drive):
    centre = padded[..., 1:-1, 1:-1]
    east = padded[..., 1:-1, 2:]
    west = padded[..., 1:-1, :-2]
    north = padded[..., 2:, 1:-1]
    south = padded[..., :-2, 1:-1]
    laplace = east + west + north + south - 4.0 * centre
    grad_x = 0.5 * (east - west)
    grad_y = 0.5 * (north - south)
    theta = centre[:, 0]
    salt = centre[:, 1]
    uvel = centre[:, 2]
    vvel = centre[:, 3]
    dens_x = -thermal_coef * grad_x[:, 0] + haline_coef * grad_x[:, 1]
    dens_y = -thermal_coef * grad_y[:, 0] + haline_coef * grad_y[:, 1]
    new_theta = theta + time_step * (-(uvel * grad_x[:, 0] + vvel * grad_y[:, 0]) + diffuse_rate * laplace[:, 0] + vertical_mix * level_mix(theta))
    new_salt = salt + time_step * (-(uvel * grad_x[:, 1] + vvel * grad_y[:, 1]) + diffuse_rate * laplace[:, 1] + vertical_mix * level_mix(salt))
    new_u = uvel + time_step * (viscosity * laplace[:, 2] + coriolis * vvel - buoyancy_scale * dens_x - drag_rate * uvel)
    new_v = vvel + time_step * (viscosity * laplace[:, 3] - coriolis * uvel - buoyancy_scale * dens_y - drag_rate * vvel)
    result = jnp.stack([new_theta, new_salt, new_u, new_v], axis=1)
    result = result.at[:, :, 0].add(time_step * drive)
    return result * mask[:, None]

def fill_halo(field, neighbour, rotation):
    strips = edge_strips(field)
    valid = neighbour >= 0
    source = jnp.maximum(neighbour, 0).astype(jnp.int32)
    side = (rotation % 4).astype(jnp.int32)
    flip = rotation // 4
    chosen = strips[source, side]
    flipped = jnp.where((flip == 1)[..., None, None, None], chosen[..., ::-1], chosen)
    halos = jnp.where(valid[..., None, None, None], flipped, jnp.zeros_like(flipped))
    return place_halo(field, halos)

def reference(state, forcing, cotangent, neighbour, rotation, wet, levels):
    depth = jnp.arange(LEVELS, dtype=jnp.int32)[None, :, None, None]
    mask = ((depth < levels[:, None]) & (wet[:, None, None, None] == 1)).astype(jnp.float32)

    def forward(start, drive):
        field = start * mask[:, None]
        for moment in range(STEPS):
            field = step_tiles(fill_halo(field, neighbour, rotation), mask, drive[:, moment])
        return field
    final_state, pullback = jax.vjp(forward, state, forcing)
    state_gradient, forcing_gradient = pullback(cotangent)
    return (state_gradient, forcing_gradient)
```

```python
import jax
import jax.numpy as jnp
from jax import lax
from jax.experimental import pallas as pl
from jax.experimental.pallas import tpu as pltpu
from jax.sharding import PartitionSpec as P

MESH = pl.DeviceIdType.MESH
WEST, EAST, SOUTH, NORTH = 0, 1, 2, 3
SIGN = (-1.0, 1.0, -1.0, 1.0)
TOP = 8
ROWS = 16
F32 = jnp.float32


def iota(shape, axis):
    return lax.broadcasted_iota(jnp.int32, shape, axis)


def up(x, n):
    return pltpu.roll(x, (-n) % 8, 0)


def lift(x, side):
    row = iota((8, 128), 0)
    near, far = (2, 4) if side < 2 else (4, 6)
    return jnp.where(row < 2, up(x, far), jnp.where(row < 4, up(x, near), 0.0))


def lower(theta, salt, side):
    row = iota((8, 128), 0)
    first = 4 if side < 2 else 6
    here = (row >= first) & (row < first + 2)
    return jnp.where(here, up(theta, -first) + up(salt, 2 - first), 0.0)


def rim_gradient(m, x, side):
    row = iota((8, 128), 0)
    weight = jnp.where(row < 2, 0.125, -0.1)
    return m * (0.15 - 0.5 * SIGN[side] * lift(x, side)) + SIGN[side] * weight * lift(m, side)


def rim_step(halo, x, side):
    pressure = lower(0.125 * halo, -0.1 * halo, side)
    return halo * (0.15 - 0.5 * SIGN[side] * lift(x, side)) + SIGN[side] * pressure


def rim_velocity(m, halo, side):
    product = m * halo
    return -0.5 * SIGN[side] * lower(product, product, side)


def crossed(c):
    lane = iota((8, 128), 1)
    first, last = lane == 0, lane == 127

    def at(low, high):
        return jnp.where(first, low, jnp.where(last, high, 0.0))

    right = [pltpu.roll(v, 1, 1) for v in c]
    left = [pltpu.roll(v, 127, 1) for v in c]
    return [
        c[WEST] + at(c[SOUTH], left[NORTH]),
        c[EAST] + at(right[SOUTH], c[NORTH]),
        c[SOUTH] + at(c[WEST], left[EAST]),
        c[NORTH] + at(right[WEST], c[EAST]),
    ]


def from_west(x):
    return jnp.where(iota(x.shape, 1) == 0, 0.0, pltpu.roll(x, 1, 1))


def from_east(x):
    return jnp.where(iota(x.shape, 1) == 127, 0.0, pltpu.roll(x, 127, 1))


def pick_columns(planes):
    lane = iota(planes[0].shape, 1)
    out = jnp.zeros_like(planes[0])
    for p, x in enumerate(planes):
        out = jnp.where(lane == p, pltpu.roll(x, p, 1) if p else x, out)
        out = jnp.where(lane == 8 + p, pltpu.roll(x, 9 + p, 1), out)
    return out


def put_columns(columns, p):
    lane = iota(columns.shape, 1)
    west = pltpu.roll(columns, 128 - p, 1) if p else columns
    east = pltpu.roll(columns, 119 - p, 1)
    return jnp.where(lane == 0, west, jnp.where(lane == 127, east, 0.0))


def step_block(xp, drive, mask, r):
    def at(p, shift=0):
        return xp[p, TOP + r + shift : TOP + r + shift + ROWS, :]

    out = [None] * 8
    for l in range(2):
        c = [at(2 * f + l) for f in range(4)]
        other = [at(2 * f + 1 - l) for f in range(2)]
        new = []
        grads = []
        for f in range(4):
            e, w = from_east(c[f]), from_west(c[f])
            n, s = at(2 * f + l, 1), at(2 * f + l, -1)
            lap = e + w + n + s - 4.0 * c[f]
            grads.append((0.5 * (e - w), 0.5 * (n - s)))
            new.append(c[f] + 0.15 * lap)
        u, v = c[2], c[3]
        for f in range(2):
            new[f] = new[f] - (u * grads[f][0] + v * grads[f][1]) + 0.1 * (other[f] - c[f])
        new[2] = new[2] + 0.3 * v - 0.25 * (0.8 * grads[1][0] - grads[0][0]) - 0.05 * u
        new[3] = new[3] - 0.3 * u - 0.25 * (0.8 * grads[1][1] - grads[0][1]) - 0.05 * v
        for f in range(4):
            if l == 0:
                new[f] = new[f] + drive[f, r : r + ROWS, :]
            out[2 * f + l] = new[f] * mask[l, r : r + ROWS, :]
    return out


def back_block(xp, mp, r):
    def x_at(p, shift=0):
        return xp[p, TOP + r + shift : TOP + r + shift + ROWS, :]

    def m_at(p, shift=0):
        return mp[p, TOP + r + shift : TOP + r + shift + ROWS, :]

    out = [None] * 8
    for l in range(2):
        u = 0.5 * x_at(4 + l)
        v_s, v_n = 0.5 * x_at(6 + l, -1), 0.5 * x_at(6 + l, 1)
        c, d = m_at(4 + l), m_at(6 + l)
        c_s, c_n, d_s, d_n = m_at(4 + l, -1), m_at(4 + l, 1), m_at(6 + l, -1), m_at(6 + l, 1)
        g_u = 0.15 * (from_west(c) + from_east(c) + c_s + c_n) + 0.35 * c - 0.3 * d
        g_v = 0.15 * (from_west(d) + from_east(d) + d_s + d_n) + 0.35 * d + 0.3 * c
        for f, k in ((0, 0.125), (1, -0.1)):
            p = 2 * f + l
            a, a_s, a_n, a_o = m_at(p), m_at(p, -1), m_at(p, 1), m_at(2 * f + 1 - l)
            kc = k * c
            au = a * u
            a15 = 0.15 * a
            g = from_west(a15 - au + kc) + from_east(a15 + au - kc)
            g = g + a_s * (0.15 - v_s) + a_n * (0.15 + v_n) + k * (d_s - d_n)
            out[p] = g + 0.3 * a + 0.1 * a_o
            x = x_at(p)
            half = 0.5 * a
            g_u = g_u - half * (from_east(x) - from_west(x))
            g_v = g_v - half * (x_at(p, 1) - x_at(p, -1))
        out[4 + l], out[6 + l] = g_u, g_v
    return out


def kernel(
    nb, rot, wet, state, forcing, cot, levels, sg_out, fg_out,
    st, drive, ctv, lev, mask, x0p, x1p, m2p, m1p, part, sgv, fgv, cols,
    a_send, a_recv, t_send, t_recv,
    bg_send, bl_send, bu_send, bg_recv, bf_recv,
    dg_send, dl_send, du_send, dg_recv, df_recv,
    in_sem, out_sem, send_sem, recv_sem,
):
    group, faces = lax.axis_size("tile"), lax.axis_size("face")
    face, tile = lax.axis_index("face"), lax.axis_index("tile")
    below, above = lax.rem(face + faces - 1, faces), lax.rem(face + 1, faces)
    peers = [lax.rem(tile + j, group) for j in range(1, group)]
    me = face * group + tile
    blocks = range(0, 128, ROWS)

    loads = [
        pltpu.make_async_copy(state.at[0], st, in_sem.at[0]),
        pltpu.make_async_copy(levels.at[0], lev, in_sem.at[1]),
        pltpu.make_async_copy(cot.at[0], ctv, in_sem.at[2]),
        pltpu.make_async_copy(forcing.at[0, 0], drive, in_sem.at[3]),
    ]
    for load in loads:
        load.start()
    barrier = pltpu.get_barrier_semaphore()
    for peer in peers:
        pl.semaphore_signal(barrier, inc=1, device_id=(face, peer), device_id_type=MESH)
    for other in (below, above):
        pl.semaphore_signal(barrier, inc=1, device_id=(other, tile), device_id_type=MESH)

    pad = jnp.zeros((8, TOP, 128), F32)
    for ref in (x0p, x1p, m2p, m1p):
        ref[:, 0:TOP, :] = pad
        ref[:, TOP + 128 : 2 * TOP + 128, :] = pad

    side_of = [lax.rem(rot[0, k], 4) for k in range(4)]
    flip = [rot[0, k] >= 4 for k in range(4)]
    source = [nb[0, k] for k in range(4)]
    valid = [s >= 0 for s in source]
    source_tile = [lax.rem(jnp.maximum(s, 0), group) for s in source]
    code = [jnp.where(valid[k], source[k] * 4 + side_of[k], -1) for k in range(4)]
    is_wet = wet[0] == 1
    lane = iota((8, 128), 1)
    row = iota((8, 128), 0)

    def turn(x, k):
        back = jnp.take_along_axis(x, 127 - lane, axis=1)
        return jnp.where(flip[k], back, x)

    table = jnp.full((8, 128), -1, jnp.int32)
    for k in range(4):
        table = jnp.where(row == k, code[k], table)
    t_send[...] = table
    t_recv[tile] = table

    def send(phase, to_peer, to_below, to_above):
        copies = []
        for j, peer in reversed(list(enumerate(peers))):
            src, dst = to_peer
            copies.append(
                pltpu.make_async_remote_copy(
                    src, dst, send_sem.at[phase, j], recv_sem.at[phase, tile],
                    device_id=(face, peer), device_id_type=MESH,
                )
            )
        for j, (src, dst), other, slot in (
            (group - 1, to_below, below, group + 1),
            (group, to_above, above, group),
        ):
            copies.append(
                pltpu.make_async_remote_copy(
                    src, dst, send_sem.at[phase, j], recv_sem.at[phase, slot],
                    device_id=(other, tile), device_id_type=MESH,
                )
            )
        for copy in copies:
            copy.start()
        return copies

    def receive(phase, from_peer, from_below, from_above):
        for j, peer in enumerate(peers):
            ref = from_peer(peer)
            pltpu.make_async_remote_copy(
                ref, ref, send_sem.at[phase, j], recv_sem.at[phase, peer],
                device_id=(face, peer), device_id_type=MESH,
            ).wait_recv()
        for ref, slot, other in ((from_below, group, below), (from_above, group + 1, above)):
            pltpu.make_async_remote_copy(
                ref, ref, send_sem.at[phase, group], recv_sem.at[phase, slot],
                device_id=(other, tile), device_id_type=MESH,
            ).wait_recv()

    loads[1].wait()
    loads[0].wait()
    for r in blocks:
        deep = jnp.where(is_wet, lev[r : r + ROWS, :], 0)
        masks = [(deep > l).astype(F32) for l in range(2)]
        planes = []
        for l in range(2):
            mask[l, r : r + ROWS, :] = masks[l]
        for p in range(8):
            x = st[p // 2, p % 2, r : r + ROWS, :] * masks[p % 2]
            x0p[p, TOP + r : TOP + r + ROWS, :] = x
            planes.append(x)
        picked = pick_columns(planes)
        wide = iota(picked.shape, 1)
        for l in range(2):
            picked = jnp.where(wide == 16 + l, pltpu.roll(masks[l], 16 + l, 1), picked)
            picked = jnp.where(wide == 18 + l, pltpu.roll(masks[l], 19 + l, 1), picked)
        cols[0, r : r + ROWS, :] = picked

    def even_odd(even, odd):
        return jnp.where(
            lax.rem(row, 2) == 0, jnp.broadcast_to(even, (8, 128)), jnp.broadcast_to(odd, (8, 128))
        )

    def rows_of(ref, at):
        return jnp.concatenate([ref[p, at : at + 1, :] for p in range(8)], axis=0)

    turned = jnp.transpose(cols[0])
    x0 = [turned[0:8], turned[8:16], rows_of(x0p, TOP), rows_of(x0p, TOP + 127)]
    rim_mask = [
        even_odd(turned[16:17], turned[17:18]),
        even_odd(turned[18:19], turned[19:20]),
        even_odd(mask[0, 0:1, :], mask[1, 0:1, :]),
        even_odd(mask[0, 127:128, :], mask[1, 127:128, :]),
    ]
    for k in range(4):
        a_send[k] = x0[k]
        a_recv[tile, k] = x0[k]
    pl.semaphore_wait(barrier, group + 1)
    copies = send(
        0, (a_send, a_recv.at[tile]), (a_send, a_recv.at[group + 1]), (a_send, a_recv.at[group])
    )
    copies += send(
        1, (t_send, t_recv.at[tile]), (t_send, t_recv.at[group + 1]), (t_send, t_recv.at[group])
    )

    loads[2].wait()
    for r in blocks:
        planes = []
        for p in range(8):
            m = ctv[p // 2, p % 2, r : r + ROWS, :] * mask[p % 2, r : r + ROWS, :]
            m2p[p, TOP + r : TOP + r + ROWS, :] = m
            if p % 2 == 0:
                fgv[1, p // 2, r : r + ROWS, :] = m
            planes.append(m)
        cols[1, r : r + ROWS, :] = pick_columns(planes)
    fg_second = pltpu.make_async_copy(fgv.at[1], fg_out.at[0, 1], out_sem.at[0])
    fg_second.start()
    loads[3].wait()
    for r in blocks:
        planes = step_block(x0p, drive, mask, r)
        for p in range(8):
            x1p[p, TOP + r : TOP + r + ROWS, :] = planes[p]
        cols[2, r : r + ROWS, :] = pick_columns(planes)
    turned = jnp.transpose(cols[1])
    m2 = [turned[0:8], turned[8:16], rows_of(m2p, TOP), rows_of(m2p, TOP + 127)]
    turned = jnp.transpose(cols[2])
    x1 = [turned[0:8], turned[8:16], rows_of(x1p, TOP), rows_of(x1p, TOP + 127)]

    receive(0, lambda t: a_recv.at[t], a_recv.at[group], a_recv.at[group + 1])
    place = [group, group + 1, source_tile[SOUTH], source_tile[NORTH]]

    def usable(x, k):
        return x if k < 2 else jnp.where(valid[k], x, 0.0)

    halo0 = [usable(turn(a_recv[place[k], side_of[k]], k), k) for k in range(4)]
    fix1 = [rim_mask[k] * rim_step(halo0[k], x0[k], k) for k in range(4)]
    more = crossed(fix1)
    x1 = [x1[k] + more[k] for k in range(4)]
    back2 = [turn(rim_gradient(m2[k], x1[k], k), k) for k in range(4)]
    pairs = [
        jnp.where(row < 4, x1[WEST], up(x1[EAST], 4)),
        jnp.where(row < 4, x1[SOUTH], up(x1[NORTH], 4)),
    ]
    for i, value in enumerate(pairs + [back2[SOUTH], back2[NORTH]]):
        bg_send[i] = value
        bg_recv[tile, i] = value
    for i, value in enumerate(pairs + [back2[WEST]]):
        bl_send[i] = value
    for i, value in enumerate(pairs + [back2[EAST]]):
        bu_send[i] = value
    copies += send(2, (bg_send, bg_recv.at[tile]), (bl_send, bf_recv.at[1]), (bu_send, bf_recv.at[0]))

    def put_rims(fix, index, add):
        tall = jnp.concatenate([fix[WEST], fix[EAST], jnp.zeros((112, 128), F32)], axis=0)
        cols[index] = jnp.transpose(tall)
        for p in range(8):
            add(p, 0, 1, fix[SOUTH][p : p + 1])
            add(p, 127, 1, fix[NORTH][p : p + 1])

    def add_x1(p, r, n, value):
        x1p[p, TOP + r : TOP + r + n, :] = x1p[p, TOP + r : TOP + r + n, :] + value

    put_rims(fix1, 3, add_x1)
    for r in blocks:
        columns = cols[3, r : r + ROWS, :]
        for p in range(8):
            add_x1(p, r, ROWS, put_columns(columns, p))
    for r in blocks:
        planes = back_block(x1p, m2p, r)
        for p in range(8):
            part[p, r : r + ROWS, :] = planes[p]
        cols[4, r : r + ROWS, :] = pick_columns(planes)
    turned = jnp.transpose(cols[4])
    g1 = [turned[0:8], turned[8:16], rows_of(part, 0), rows_of(part, 127)]

    receive(1, lambda t: t_recv.at[t], t_recv.at[group], t_recv.at[group + 1])
    receive(2, lambda t: bg_recv.at[t], bf_recv.at[0], bf_recv.at[1])

    def pair(ref, at, k):
        both = ref[at, lax.div(side_of[k], 2)]
        return jnp.where(lax.rem(side_of[k], 2) == 1, up(both, 4), both)

    halo1 = [
        pair(bf_recv, 0, WEST), pair(bf_recv, 1, EAST),
        pair(bg_recv, source_tile[SOUTH], SOUTH), pair(bg_recv, source_tile[NORTH], NORTH),
    ]
    halo1 = [usable(turn(halo1[k], k), k) for k in range(4)]

    senders = [(t, k) for t in range(group) for k in (SOUTH, NORTH)] + [(group, EAST), (group + 1, WEST)]
    codes = [jnp.broadcast_to(t_recv[t, k : k + 1, :], (8, 128)) for t, k in senders]

    def returned(values, k):
        total = jnp.zeros((8, 128), F32)
        for seen, value in zip(codes, values):
            total = total + jnp.where(seen == me * 4 + k, value, 0.0)
        return total

    values = [bg_recv[t, k] for t in range(group) for k in (2, 3)] + [bf_recv[0, 2], bf_recv[1, 2]]
    fix2 = [rim_velocity(m2[k], halo1[k], k) + returned(values, k) for k in range(4)]
    more = crossed(fix2)
    m1 = [rim_mask[k] * (g1[k] + more[k]) for k in range(4)]
    back1 = [turn(rim_gradient(m1[k], x0[k], k), k) for k in range(4)]
    for i, k in enumerate((SOUTH, NORTH)):
        dg_send[i] = back1[k]
        dg_recv[tile, i] = back1[k]
    dl_send[0] = back1[WEST]
    du_send[0] = back1[EAST]
    copies += send(3, (dg_send, dg_recv.at[tile]), (dl_send, df_recv.at[1]), (du_send, df_recv.at[0]))

    def add_part(p, r, n, value):
        part[p, r : r + n, :] = part[p, r : r + n, :] + value

    put_rims(fix2, 5, add_part)
    for r in blocks:
        columns = cols[5, r : r + ROWS, :]
        for p in range(8):
            m = part[p, r : r + ROWS, :] + put_columns(columns, p)
            m = m * mask[p % 2, r : r + ROWS, :]
            m1p[p, TOP + r : TOP + r + ROWS, :] = m
            if p % 2 == 0:
                fgv[0, p // 2, r : r + ROWS, :] = m
    fg_first = pltpu.make_async_copy(fgv.at[0], fg_out.at[0, 0], out_sem.at[1])
    fg_first.start()
    for r in blocks:
        planes = back_block(x0p, m1p, r)
        for p in range(8):
            part[p, r : r + ROWS, :] = planes[p] * mask[p % 2, r : r + ROWS, :]
    own = [rim_velocity(m1[k], halo0[k], k) for k in range(4)]

    receive(3, lambda t: dg_recv.at[t], df_recv.at[0], df_recv.at[1])
    values = [dg_recv[t, i] for t in range(group) for i in (0, 1)] + [df_recv[0, 0], df_recv[1, 0]]
    fix3 = [rim_mask[k] * (own[k] + returned(values, k)) for k in range(4)]
    put_rims(fix3, 6, add_part)
    for r in blocks:
        columns = cols[6, r : r + ROWS, :]
        for p in range(8):
            sgv[p // 2, p % 2, r : r + ROWS, :] = part[p, r : r + ROWS, :] + put_columns(columns, p)
    sg_copy = pltpu.make_async_copy(sgv, sg_out.at[0], out_sem.at[2])
    sg_copy.start()
    for copy in copies:
        copy.wait_send()
    fg_second.wait()
    fg_first.wait()
    sg_copy.wait()


def shards(state, forcing, cotangent, neighbour, rotation, wet, levels):
    group = lax.axis_size("tile")
    anywhere = pl.BlockSpec(memory_space=pl.ANY)
    scalars = pl.BlockSpec(memory_space=pltpu.SMEM)
    fields, depth, side = state.shape[1], state.shape[2], state.shape[3]
    vm = lambda *shape: pltpu.VMEM(shape, F32)
    whole = lambda *shape: pltpu.VMEM(shape, jnp.int32)
    padded = vm(8, side + 2 * TOP, side)
    return pl.pallas_call(
        kernel,
        out_shape=(
            jax.ShapeDtypeStruct(state.shape, F32),
            jax.ShapeDtypeStruct(forcing.shape, F32),
        ),
        in_specs=[scalars] * 3 + [anywhere] * 4,
        out_specs=(anywhere, anywhere),
        scratch_shapes=[
            vm(fields, depth, side, side), vm(fields, side, side), vm(fields, depth, side, side),
            whole(side, side), vm(depth, side, side),
            padded, padded, padded, padded,
            vm(8, side, side), vm(fields, depth, side, side), vm(2, fields, side, side),
            vm(7, side, side),
            vm(4, 8, side), vm(group + 2, 4, 8, side),
            whole(8, side), whole(group + 2, 8, side),
            vm(4, 8, side), vm(3, 8, side), vm(3, 8, side), vm(group, 4, 8, side), vm(2, 3, 8, side),
            vm(2, 8, side), vm(1, 8, side), vm(1, 8, side), vm(group, 2, 8, side), vm(2, 1, 8, side),
            pltpu.SemaphoreType.DMA((4,)), pltpu.SemaphoreType.DMA((3,)),
            pltpu.SemaphoreType.DMA((4, group + 1)), pltpu.SemaphoreType.DMA((4, group + 2)),
        ],
        compiler_params=pltpu.CompilerParams(
            collective_id=0, has_side_effects=True, vmem_limit_bytes=32 * 1024 * 1024
        ),
        name="window",
    )(neighbour, rotation, wet, state, forcing, cotangent, levels)


def solution(mesh):
    placed = (
        P(("face", "tile"), None, None, None, None),
        P(("face", "tile"), None, None, None, None),
        P(("face", "tile"), None, None, None, None),
        P(("face", "tile"), None),
        P(("face", "tile"), None),
        P(("face", "tile")),
        P(("face", "tile"), None, None),
    )
    return jax.shard_map(
        shards,
        mesh=mesh,
        in_specs=placed,
        out_specs=(
            P(("face", "tile"), None, None, None, None),
            P(("face", "tile"), None, None, None, None),
        ),
        check_vma=False,
    )
```

```python
import jax
import jax.numpy as jnp
from jax import lax
from jax.experimental import pallas as pl
from jax.experimental.pallas import tpu as pltpu
from jax.sharding import PartitionSpec as P

MESH = pl.DeviceIdType.MESH
WEST, EAST, SOUTH, NORTH = 0, 1, 2, 3
SIGN = (-1.0, 1.0, -1.0, 1.0)
TOP = 8
ROWS = 16
F32 = jnp.float32


def iota(shape, axis):
    return lax.broadcasted_iota(jnp.int32, shape, axis)


def up(x, n):
    return pltpu.roll(x, (-n) % 8, 0)


def lift(x, side):
    row = iota((8, 128), 0)
    near, far = (2, 4) if side < 2 else (4, 6)
    return jnp.where(row < 2, up(x, far), jnp.where(row < 4, up(x, near), 0.0))


def lower(theta, salt, side):
    row = iota((8, 128), 0)
    first = 4 if side < 2 else 6
    here = (row >= first) & (row < first + 2)
    return jnp.where(here, up(theta, -first) + up(salt, 2 - first), 0.0)


def rim_gradient(m, x, side):
    row = iota((8, 128), 0)
    weight = jnp.where(row < 2, 0.125, -0.1)
    return m * (0.15 - 0.5 * SIGN[side] * lift(x, side)) + SIGN[side] * weight * lift(m, side)


def rim_step(halo, x, side):
    pressure = lower(0.125 * halo, -0.1 * halo, side)
    return halo * (0.15 - 0.5 * SIGN[side] * lift(x, side)) + SIGN[side] * pressure


def rim_velocity(m, halo, side):
    product = m * halo
    return -0.5 * SIGN[side] * lower(product, product, side)


def crossed(c):
    lane = iota((8, 128), 1)
    first, last = lane == 0, lane == 127

    def at(low, high):
        return jnp.where(first, low, jnp.where(last, high, 0.0))

    right = [pltpu.roll(v, 1, 1) for v in c]
    left = [pltpu.roll(v, 127, 1) for v in c]
    return [
        c[WEST] + at(c[SOUTH], left[NORTH]),
        c[EAST] + at(right[SOUTH], c[NORTH]),
        c[SOUTH] + at(c[WEST], left[EAST]),
        c[NORTH] + at(right[WEST], c[EAST]),
    ]


def from_west(x):
    return jnp.where(iota(x.shape, 1) == 0, 0.0, pltpu.roll(x, 1, 1))


def from_east(x):
    return jnp.where(iota(x.shape, 1) == 127, 0.0, pltpu.roll(x, 127, 1))


def pick_columns(planes):
    lane = iota(planes[0].shape, 1)
    out = jnp.zeros_like(planes[0])
    for p, x in enumerate(planes):
        out = jnp.where(lane == p, pltpu.roll(x, p, 1) if p else x, out)
        out = jnp.where(lane == 8 + p, pltpu.roll(x, 9 + p, 1), out)
    return out


def put_columns(columns, p):
    lane = iota(columns.shape, 1)
    west = pltpu.roll(columns, 128 - p, 1) if p else columns
    east = pltpu.roll(columns, 119 - p, 1)
    return jnp.where(lane == 0, west, jnp.where(lane == 127, east, 0.0))


def step_block(xp, drive, mask, r):
    def at(p, shift=0):
        return xp[p, TOP + r + shift : TOP + r + shift + ROWS, :]

    out = [None] * 8
    for l in range(2):
        c = [at(2 * f + l) for f in range(4)]
        other = [at(2 * f + 1 - l) for f in range(2)]
        new = []
        grads = []
        for f in range(4):
            e, w = from_east(c[f]), from_west(c[f])
            n, s = at(2 * f + l, 1), at(2 * f + l, -1)
            lap = e + w + n + s - 4.0 * c[f]
            grads.append((0.5 * (e - w), 0.5 * (n - s)))
            new.append(c[f] + 0.15 * lap)
        u, v = c[2], c[3]
        for f in range(2):
            new[f] = new[f] - (u * grads[f][0] + v * grads[f][1]) + 0.1 * (other[f] - c[f])
        new[2] = new[2] + 0.3 * v - 0.25 * (0.8 * grads[1][0] - grads[0][0]) - 0.05 * u
        new[3] = new[3] - 0.3 * u - 0.25 * (0.8 * grads[1][1] - grads[0][1]) - 0.05 * v
        for f in range(4):
            if l == 0:
                new[f] = new[f] + drive[f, r : r + ROWS, :]
            out[2 * f + l] = new[f] * mask[l, r : r + ROWS, :]
    return out


def back_block(xp, mp, r):
    def x_at(p, shift=0):
        return xp[p, TOP + r + shift : TOP + r + shift + ROWS, :]

    def m_at(p, shift=0):
        return mp[p, TOP + r + shift : TOP + r + shift + ROWS, :]

    out = [None] * 8
    for l in range(2):
        u = 0.5 * x_at(4 + l)
        v_s, v_n = 0.5 * x_at(6 + l, -1), 0.5 * x_at(6 + l, 1)
        c, d = m_at(4 + l), m_at(6 + l)
        c_s, c_n, d_s, d_n = m_at(4 + l, -1), m_at(4 + l, 1), m_at(6 + l, -1), m_at(6 + l, 1)
        g_u = 0.15 * (from_west(c) + from_east(c) + c_s + c_n) + 0.35 * c - 0.3 * d
        g_v = 0.15 * (from_west(d) + from_east(d) + d_s + d_n) + 0.35 * d + 0.3 * c
        for f, k in ((0, 0.125), (1, -0.1)):
            p = 2 * f + l
            a, a_s, a_n, a_o = m_at(p), m_at(p, -1), m_at(p, 1), m_at(2 * f + 1 - l)
            kc = k * c
            au = a * u
            a15 = 0.15 * a
            g = from_west(a15 - au + kc) + from_east(a15 + au - kc)
            g = g + a_s * (0.15 - v_s) + a_n * (0.15 + v_n) + k * (d_s - d_n)
            out[p] = g + 0.3 * a + 0.1 * a_o
            x = x_at(p)
            half = 0.5 * a
            g_u = g_u - half * (from_east(x) - from_west(x))
            g_v = g_v - half * (x_at(p, 1) - x_at(p, -1))
        out[4 + l], out[6 + l] = g_u, g_v
    return out


def kernel(
    nb, rot, wet, state, forcing, cot, levels, sg_out, fg_out,
    st, drive, ctv, lev, mask, x0p, x1p, m2p, m1p, part, sgv, fgv, cols,
    a_send, a_recv, t_send, t_recv,
    bg_send, bl_send, bu_send, bg_recv, bf_recv,
    dg_send, dl_send, du_send, dg_recv, df_recv,
    in_sem, out_sem, send_sem, recv_sem,
):
    group, faces = lax.axis_size("tile"), lax.axis_size("face")
    face, tile = lax.axis_index("face"), lax.axis_index("tile")
    below, above = lax.rem(face + faces - 1, faces), lax.rem(face + 1, faces)
    peers = [lax.rem(tile + j, group) for j in range(1, group)]
    me = face * group + tile
    blocks = range(0, 128, ROWS)

    loads = [
        pltpu.make_async_copy(state.at[0], st, in_sem.at[0]),
        pltpu.make_async_copy(levels.at[0], lev, in_sem.at[1]),
        pltpu.make_async_copy(cot.at[0], ctv, in_sem.at[2]),
        pltpu.make_async_copy(forcing.at[0, 0], drive, in_sem.at[3]),
    ]
    for load in loads:
        load.start()
    barrier = pltpu.get_barrier_semaphore()
    for peer in peers:
        pl.semaphore_signal(barrier, inc=1, device_id=(face, peer), device_id_type=MESH)
    for other in (below, above):
        pl.semaphore_signal(barrier, inc=1, device_id=(other, tile), device_id_type=MESH)

    pad = jnp.zeros((8, TOP, 128), F32)
    for ref in (x0p, x1p, m2p, m1p):
        ref[:, 0:TOP, :] = pad
        ref[:, TOP + 128 : 2 * TOP + 128, :] = pad

    side_of = [lax.rem(rot[0, k], 4) for k in range(4)]
    flip = [rot[0, k] >= 4 for k in range(4)]
    source = [nb[0, k] for k in range(4)]
    valid = [s >= 0 for s in source]
    source_tile = [lax.rem(jnp.maximum(s, 0), group) for s in source]
    code = [jnp.where(valid[k], source[k] * 4 + side_of[k], -1) for k in range(4)]
    is_wet = wet[0] == 1
    lane = iota((8, 128), 1)
    row = iota((8, 128), 0)

    def turn(x, k):
        back = jnp.take_along_axis(x, 127 - lane, axis=1)
        return jnp.where(flip[k], back, x)

    table = jnp.full((8, 128), -1, jnp.int32)
    for k in range(4):
        table = jnp.where(row == k, code[k], table)
    t_send[...] = table
    t_recv[tile] = table

    def send(phase, to_peer, to_below, to_above):
        copies = []
        for j, peer in reversed(list(enumerate(peers))):
            src, dst = to_peer
            copies.append(
                pltpu.make_async_remote_copy(
                    src, dst, send_sem.at[phase, j], recv_sem.at[phase, tile],
                    device_id=(face, peer), device_id_type=MESH,
                )
            )
        for j, (src, dst), other, slot in (
            (group - 1, to_below, below, group + 1),
            (group, to_above, above, group),
        ):
            copies.append(
                pltpu.make_async_remote_copy(
                    src, dst, send_sem.at[phase, j], recv_sem.at[phase, slot],
                    device_id=(other, tile), device_id_type=MESH,
                )
            )
        for copy in copies:
            copy.start()
        return copies

    def receive(phase, from_peer, from_below, from_above):
        for j, peer in enumerate(peers):
            ref = from_peer(peer)
            pltpu.make_async_remote_copy(
                ref, ref, send_sem.at[phase, j], recv_sem.at[phase, peer],
                device_id=(face, peer), device_id_type=MESH,
            ).wait_recv()
        for ref, slot, other in ((from_below, group, below), (from_above, group + 1, above)):
            pltpu.make_async_remote_copy(
                ref, ref, send_sem.at[phase, group], recv_sem.at[phase, slot],
                device_id=(other, tile), device_id_type=MESH,
            ).wait_recv()

    loads[1].wait()
    loads[0].wait()
    for r in blocks:
        deep = jnp.where(is_wet, lev[r : r + ROWS, :], 0)
        masks = [(deep > l).astype(F32) for l in range(2)]
        planes = []
        for l in range(2):
            mask[l, r : r + ROWS, :] = masks[l]
        for p in range(8):
            x = st[p // 2, p % 2, r : r + ROWS, :] * masks[p % 2]
            x0p[p, TOP + r : TOP + r + ROWS, :] = x
            planes.append(x)
        picked = pick_columns(planes)
        wide = iota(picked.shape, 1)
        for l in range(2):
            picked = jnp.where(wide == 16 + l, pltpu.roll(masks[l], 16 + l, 1), picked)
            picked = jnp.where(wide == 18 + l, pltpu.roll(masks[l], 19 + l, 1), picked)
        cols[0, r : r + ROWS, :] = picked

    def even_odd(even, odd):
        return jnp.where(
            lax.rem(row, 2) == 0, jnp.broadcast_to(even, (8, 128)), jnp.broadcast_to(odd, (8, 128))
        )

    def rows_of(ref, at):
        return jnp.concatenate([ref[p, at : at + 1, :] for p in range(8)], axis=0)

    turned = jnp.transpose(cols[0])
    x0 = [turned[0:8], turned[8:16], rows_of(x0p, TOP), rows_of(x0p, TOP + 127)]
    rim_mask = [
        even_odd(turned[16:17], turned[17:18]),
        even_odd(turned[18:19], turned[19:20]),
        even_odd(mask[0, 0:1, :], mask[1, 0:1, :]),
        even_odd(mask[0, 127:128, :], mask[1, 127:128, :]),
    ]
    for k in range(4):
        a_send[k] = x0[k]
        a_recv[tile, k] = x0[k]
    pl.semaphore_wait(barrier, group + 1)
    copies = send(
        0, (a_send, a_recv.at[tile]), (a_send, a_recv.at[group + 1]), (a_send, a_recv.at[group])
    )
    copies += send(
        1, (t_send, t_recv.at[tile]), (t_send, t_recv.at[group + 1]), (t_send, t_recv.at[group])
    )

    loads[2].wait()
    for r in blocks:
        planes = []
        for p in range(8):
            m = ctv[p // 2, p % 2, r : r + ROWS, :] * mask[p % 2, r : r + ROWS, :]
            m2p[p, TOP + r : TOP + r + ROWS, :] = m
            if p % 2 == 0:
                fgv[1, p // 2, r : r + ROWS, :] = m
            planes.append(m)
        cols[1, r : r + ROWS, :] = pick_columns(planes)
    fg_second = pltpu.make_async_copy(fgv.at[1], fg_out.at[0, 1], out_sem.at[0])
    fg_second.start()
    loads[3].wait()
    for r in blocks:
        planes = step_block(x0p, drive, mask, r)
        for p in range(8):
            x1p[p, TOP + r : TOP + r + ROWS, :] = planes[p]
        cols[2, r : r + ROWS, :] = pick_columns(planes)
    turned = jnp.transpose(cols[1])
    m2 = [turned[0:8], turned[8:16], rows_of(m2p, TOP), rows_of(m2p, TOP + 127)]
    turned = jnp.transpose(cols[2])
    x1 = [turned[0:8], turned[8:16], rows_of(x1p, TOP), rows_of(x1p, TOP + 127)]

    receive(0, lambda t: a_recv.at[t], a_recv.at[group], a_recv.at[group + 1])
    place = [group, group + 1, source_tile[SOUTH], source_tile[NORTH]]

    def usable(x, k):
        return x if k < 2 else jnp.where(valid[k], x, 0.0)

    halo0 = [usable(turn(a_recv[place[k], side_of[k]], k), k) for k in range(4)]
    fix1 = [rim_mask[k] * rim_step(halo0[k], x0[k], k) for k in range(4)]
    more = crossed(fix1)
    x1 = [x1[k] + more[k] for k in range(4)]
    back2 = [turn(rim_gradient(m2[k], x1[k], k), k) for k in range(4)]
    pairs = [
        jnp.where(row < 4, x1[WEST], up(x1[EAST], 4)),
        jnp.where(row < 4, x1[SOUTH], up(x1[NORTH], 4)),
    ]
    for i, value in enumerate(pairs + [back2[SOUTH], back2[NORTH]]):
        bg_send[i] = value
        bg_recv[tile, i] = value
    for i, value in enumerate(pairs + [back2[WEST]]):
        bl_send[i] = value
    for i, value in enumerate(pairs + [back2[EAST]]):
        bu_send[i] = value
    copies += send(2, (bg_send, bg_recv.at[tile]), (bl_send, bf_recv.at[1]), (bu_send, bf_recv.at[0]))

    def put_rims(fix, index, add):
        tall = jnp.concatenate([fix[WEST], fix[EAST], jnp.zeros((112, 128), F32)], axis=0)
        cols[index] = jnp.transpose(tall)
        for p in range(8):
            add(p, 0, 1, fix[SOUTH][p : p + 1])
            add(p, 127, 1, fix[NORTH][p : p + 1])

    def add_x1(p, r, n, value):
        x1p[p, TOP + r : TOP + r + n, :] = x1p[p, TOP + r : TOP + r + n, :] + value

    put_rims(fix1, 3, add_x1)
    for r in blocks:
        columns = cols[3, r : r + ROWS, :]
        for p in range(8):
            add_x1(p, r, ROWS, put_columns(columns, p))
    for r in blocks:
        planes = back_block(x1p, m2p, r)
        for p in range(8):
            part[p, r : r + ROWS, :] = planes[p]
        cols[4, r : r + ROWS, :] = pick_columns(planes)
    turned = jnp.transpose(cols[4])
    g1 = [turned[0:8], turned[8:16], rows_of(part, 0), rows_of(part, 127)]

    receive(1, lambda t: t_recv.at[t], t_recv.at[group], t_recv.at[group + 1])
    receive(2, lambda t: bg_recv.at[t], bf_recv.at[0], bf_recv.at[1])

    def pair(ref, at, k):
        both = ref[at, lax.div(side_of[k], 2)]
        return jnp.where(lax.rem(side_of[k], 2) == 1, up(both, 4), both)

    halo1 = [
        pair(bf_recv, 0, WEST), pair(bf_recv, 1, EAST),
        pair(bg_recv, source_tile[SOUTH], SOUTH), pair(bg_recv, source_tile[NORTH], NORTH),
    ]
    halo1 = [usable(turn(halo1[k], k), k) for k in range(4)]

    senders = [(t, k) for t in range(group) for k in (SOUTH, NORTH)] + [(group, EAST), (group + 1, WEST)]
    codes = [jnp.broadcast_to(t_recv[t, k : k + 1, :], (8, 128)) for t, k in senders]

    def returned(values, k):
        total = jnp.zeros((8, 128), F32)
        for seen, value in zip(codes, values):
            total = total + jnp.where(seen == me * 4 + k, value, 0.0)
        return total

    values = [bg_recv[t, k] for t in range(group) for k in (2, 3)] + [bf_recv[0, 2], bf_recv[1, 2]]
    fix2 = [rim_velocity(m2[k], halo1[k], k) + returned(values, k) for k in range(4)]
    more = crossed(fix2)
    m1 = [rim_mask[k] * (g1[k] + more[k]) for k in range(4)]
    back1 = [turn(rim_gradient(m1[k], x0[k], k), k) for k in range(4)]
    for i, k in enumerate((SOUTH, NORTH)):
        dg_send[i] = back1[k]
        dg_recv[tile, i] = back1[k]
    dl_send[0] = back1[WEST]
    du_send[0] = back1[EAST]
    copies += send(3, (dg_send, dg_recv.at[tile]), (dl_send, df_recv.at[1]), (du_send, df_recv.at[0]))

    def add_part(p, r, n, value):
        part[p, r : r + n, :] = part[p, r : r + n, :] + value

    put_rims(fix2, 5, add_part)
    for r in blocks:
        columns = cols[5, r : r + ROWS, :]
        for p in range(8):
            m = part[p, r : r + ROWS, :] + put_columns(columns, p)
            m = m * mask[p % 2, r : r + ROWS, :]
            m1p[p, TOP + r : TOP + r + ROWS, :] = m
            if p % 2 == 0:
                fgv[0, p // 2, r : r + ROWS, :] = m
    fg_first = pltpu.make_async_copy(fgv.at[0], fg_out.at[0, 0], out_sem.at[1])
    fg_first.start()
    for r in blocks:
        planes = back_block(x0p, m1p, r)
        for p in range(8):
            part[p, r : r + ROWS, :] = planes[p] * mask[p % 2, r : r + ROWS, :]
    own = [rim_velocity(m1[k], halo0[k], k) for k in range(4)]

    receive(3, lambda t: dg_recv.at[t], df_recv.at[0], df_recv.at[1])
    values = [dg_recv[t, i] for t in range(group) for i in (0, 1)] + [df_recv[0, 0], df_recv[1, 0]]
    fix3 = [rim_mask[k] * (own[k] + returned(values, k)) for k in range(4)]
    put_rims(fix3, 6, add_part)
    for r in blocks:
        columns = cols[6, r : r + ROWS, :]
        for p in range(8):
            sgv[p // 2, p % 2, r : r + ROWS, :] = part[p, r : r + ROWS, :] + put_columns(columns, p)
    sg_copy = pltpu.make_async_copy(sgv, sg_out.at[0], out_sem.at[2])
    sg_copy.start()
    for copy in copies:
        copy.wait_send()
    fg_second.wait()
    fg_first.wait()
    sg_copy.wait()


def shards(state, forcing, cotangent, neighbour, rotation, wet, levels):
    group = lax.axis_size("tile")
    anywhere = pl.BlockSpec(memory_space=pl.ANY)
    scalars = pl.BlockSpec(memory_space=pltpu.SMEM)
    fields, depth, side = state.shape[1], state.shape[2], state.shape[3]
    vm = lambda *shape: pltpu.VMEM(shape, F32)
    whole = lambda *shape: pltpu.VMEM(shape, jnp.int32)
    padded = vm(8, side + 2 * TOP, side)
    return pl.pallas_call(
        kernel,
        out_shape=(
            jax.ShapeDtypeStruct(state.shape, F32),
            jax.ShapeDtypeStruct(forcing.shape, F32),
        ),
        in_specs=[scalars] * 3 + [anywhere] * 4,
        out_specs=(anywhere, anywhere),
        scratch_shapes=[
            vm(fields, depth, side, side), vm(fields, side, side), vm(fields, depth, side, side),
            whole(side, side), vm(depth, side, side),
            padded, padded, padded, padded,
            vm(8, side, side), vm(fields, depth, side, side), vm(2, fields, side, side),
            vm(7, side, side),
            vm(4, 8, side), vm(group + 2, 4, 8, side),
            whole(8, side), whole(group + 2, 8, side),
            vm(4, 8, side), vm(3, 8, side), vm(3, 8, side), vm(group, 4, 8, side), vm(2, 3, 8, side),
            vm(2, 8, side), vm(1, 8, side), vm(1, 8, side), vm(group, 2, 8, side), vm(2, 1, 8, side),
            pltpu.SemaphoreType.DMA((4,)), pltpu.SemaphoreType.DMA((3,)),
            pltpu.SemaphoreType.DMA((4, group + 1)), pltpu.SemaphoreType.DMA((4, group + 2)),
        ],
        compiler_params=pltpu.CompilerParams(
            collective_id=0, has_side_effects=True, vmem_limit_bytes=60 * 1024 * 1024
        ),
        name="window",
    )(neighbour, rotation, wet, state, forcing, cotangent, levels)


def solution(mesh):
    placed = (
        P(("face", "tile"), None, None, None, None),
        P(("face", "tile"), None, None, None, None),
        P(("face", "tile"), None, None, None, None),
        P(("face", "tile"), None),
        P(("face", "tile"), None),
        P(("face", "tile")),
        P(("face", "tile"), None, None),
    )
    return jax.shard_map(
        shards,
        mesh=mesh,
        in_specs=placed,
        out_specs=(
            P(("face", "tile"), None, None, None, None),
            P(("face", "tile"), None, None, None, None),
        ),
        check_vma=False,
    )
```

```python
import jax
import jax.numpy as jnp
from jax import lax
from jax.experimental import pallas as pl
from jax.experimental.pallas import tpu as pltpu
from jax.sharding import PartitionSpec as P

MESH = pl.DeviceIdType.MESH
WEST, EAST, SOUTH, NORTH = 0, 1, 2, 3
SIGN = (-1.0, 1.0, -1.0, 1.0)
TOP = 8
ROWS = 16
F32 = jnp.float32


def iota(shape, axis):
    return lax.broadcasted_iota(jnp.int32, shape, axis)


def up(x, n):
    return pltpu.roll(x, (-n) % 8, 0)


def lift(x, side):
    row = iota((8, 128), 0)
    near, far = (2, 4) if side < 2 else (4, 6)
    return jnp.where(row < 2, up(x, far), jnp.where(row < 4, up(x, near), 0.0))


def lower(theta, salt, side):
    row = iota((8, 128), 0)
    first = 4 if side < 2 else 6
    here = (row >= first) & (row < first + 2)
    return jnp.where(here, up(theta, -first) + up(salt, 2 - first), 0.0)


def rim_gradient(m, x, side):
    row = iota((8, 128), 0)
    weight = jnp.where(row < 2, 0.125, -0.1)
    return m * (0.15 - 0.5 * SIGN[side] * lift(x, side)) + SIGN[side] * weight * lift(m, side)


def rim_step(halo, x, side):
    pressure = lower(0.125 * halo, -0.1 * halo, side)
    return halo * (0.15 - 0.5 * SIGN[side] * lift(x, side)) + SIGN[side] * pressure


def rim_velocity(m, halo, side):
    product = m * halo
    return -0.5 * SIGN[side] * lower(product, product, side)


def crossed(c):
    lane = iota((8, 128), 1)
    first, last = lane == 0, lane == 127

    def at(low, high):
        return jnp.where(first, low, jnp.where(last, high, 0.0))

    right = [pltpu.roll(v, 1, 1) for v in c]
    left = [pltpu.roll(v, 127, 1) for v in c]
    return [
        c[WEST] + at(c[SOUTH], left[NORTH]),
        c[EAST] + at(right[SOUTH], c[NORTH]),
        c[SOUTH] + at(c[WEST], left[EAST]),
        c[NORTH] + at(right[WEST], c[EAST]),
    ]


def from_west(x):
    return jnp.where(iota(x.shape, 1) == 0, 0.0, pltpu.roll(x, 1, 1))


def from_east(x):
    return jnp.where(iota(x.shape, 1) == 127, 0.0, pltpu.roll(x, 127, 1))


def pick_columns(planes):
    lane = iota(planes[0].shape, 1)
    out = jnp.zeros_like(planes[0])
    for p, x in enumerate(planes):
        out = jnp.where(lane == p, pltpu.roll(x, p, 1) if p else x, out)
        out = jnp.where(lane == 8 + p, pltpu.roll(x, 9 + p, 1), out)
    return out


def put_columns(columns, p):
    lane = iota(columns.shape, 1)
    west = pltpu.roll(columns, 128 - p, 1) if p else columns
    east = pltpu.roll(columns, 119 - p, 1)
    return jnp.where(lane == 0, west, jnp.where(lane == 127, east, 0.0))


def step_block(xp, drive, mask, r):
    def at(p, shift=0):
        return xp[p, TOP + r + shift : TOP + r + shift + ROWS, :]

    out = [None] * 8
    for l in range(2):
        c = [at(2 * f + l) for f in range(4)]
        other = [at(2 * f + 1 - l) for f in range(2)]
        new = []
        grads = []
        for f in range(4):
            e, w = from_east(c[f]), from_west(c[f])
            n, s = at(2 * f + l, 1), at(2 * f + l, -1)
            lap = e + w + n + s - 4.0 * c[f]
            grads.append((0.5 * (e - w), 0.5 * (n - s)))
            new.append(c[f] + 0.15 * lap)
        u, v = c[2], c[3]
        for f in range(2):
            new[f] = new[f] - (u * grads[f][0] + v * grads[f][1]) + 0.1 * (other[f] - c[f])
        new[2] = new[2] + 0.3 * v - 0.25 * (0.8 * grads[1][0] - grads[0][0]) - 0.05 * u
        new[3] = new[3] - 0.3 * u - 0.25 * (0.8 * grads[1][1] - grads[0][1]) - 0.05 * v
        for f in range(4):
            if l == 0:
                new[f] = new[f] + drive[f, r : r + ROWS, :]
            out[2 * f + l] = new[f] * mask[l, r : r + ROWS, :]
    return out


def back_block(xp, mp, r):
    def x_at(p, shift=0):
        return xp[p, TOP + r + shift : TOP + r + shift + ROWS, :]

    def m_at(p, shift=0):
        return mp[p, TOP + r + shift : TOP + r + shift + ROWS, :]

    out = [None] * 8
    for l in range(2):
        u = 0.5 * x_at(4 + l)
        v_s, v_n = 0.5 * x_at(6 + l, -1), 0.5 * x_at(6 + l, 1)
        c, d = m_at(4 + l), m_at(6 + l)
        c_s, c_n, d_s, d_n = m_at(4 + l, -1), m_at(4 + l, 1), m_at(6 + l, -1), m_at(6 + l, 1)
        g_u = 0.15 * (from_west(c) + from_east(c) + c_s + c_n) + 0.35 * c - 0.3 * d
        g_v = 0.15 * (from_west(d) + from_east(d) + d_s + d_n) + 0.35 * d + 0.3 * c
        for f, k in ((0, 0.125), (1, -0.1)):
            p = 2 * f + l
            a, a_s, a_n, a_o = m_at(p), m_at(p, -1), m_at(p, 1), m_at(2 * f + 1 - l)
            kc = k * c
            au = a * u
            a15 = 0.15 * a
            g = from_west(a15 - au + kc) + from_east(a15 + au - kc)
            g = g + a_s * (0.15 - v_s) + a_n * (0.15 + v_n) + k * (d_s - d_n)
            out[p] = g + 0.3 * a + 0.1 * a_o
            x = x_at(p)
            half = 0.5 * a
            g_u = g_u - half * (from_east(x) - from_west(x))
            g_v = g_v - half * (x_at(p, 1) - x_at(p, -1))
        out[4 + l], out[6 + l] = g_u, g_v
    return out


def kernel(
    nb, rot, wet, state, forcing, cot, levels, sg_out, fg_out,
    st, drive, ctv, lev, mask, x0p, x1p, m2p, m1p, part, sgv, fgv, cols,
    a_send, a_recv, t_send, t_recv,
    bg_send, bl_send, bu_send, bg_recv, bf_recv,
    dg_send, dl_send, du_send, dg_recv, df_recv,
    in_sem, out_sem, send_sem, recv_sem,
):
    group, faces = lax.axis_size("tile"), lax.axis_size("face")
    face, tile = lax.axis_index("face"), lax.axis_index("tile")
    below, above = lax.rem(face + faces - 1, faces), lax.rem(face + 1, faces)
    peers = [lax.rem(tile + j, group) for j in range(1, group)]
    me = face * group + tile
    blocks = range(0, 128, ROWS)

    loads = [
        pltpu.make_async_copy(state.at[0], st, in_sem.at[0]),
        pltpu.make_async_copy(levels.at[0], lev, in_sem.at[1]),
        pltpu.make_async_copy(cot.at[0], ctv, in_sem.at[2]),
        pltpu.make_async_copy(forcing.at[0, 0], drive, in_sem.at[3]),
    ]
    for load in loads:
        load.start()
    barrier = pltpu.get_barrier_semaphore()
    for peer in peers:
        pl.semaphore_signal(barrier, inc=1, device_id=(face, peer), device_id_type=MESH)
    for other in (below, above):
        pl.semaphore_signal(barrier, inc=1, device_id=(other, tile), device_id_type=MESH)

    pad = jnp.zeros((8, TOP, 128), F32)
    for ref in (x0p, x1p, m2p, m1p):
        ref[:, 0:TOP, :] = pad
        ref[:, TOP + 128 : 2 * TOP + 128, :] = pad

    side_of = [lax.rem(rot[0, k], 4) for k in range(4)]
    flip = [rot[0, k] >= 4 for k in range(4)]
    source = [nb[0, k] for k in range(4)]
    valid = [s >= 0 for s in source]
    source_tile = [lax.rem(jnp.maximum(s, 0), group) for s in source]
    code = [jnp.where(valid[k], source[k] * 4 + side_of[k], -1) for k in range(4)]
    is_wet = wet[0] == 1
    lane = iota((8, 128), 1)
    row = iota((8, 128), 0)

    def turn(x, k):
        back = jnp.take_along_axis(x, 127 - lane, axis=1)
        return jnp.where(flip[k], back, x)

    table = jnp.full((8, 128), -1, jnp.int32)
    for k in range(4):
        table = jnp.where(row == k, code[k], table)
    t_send[...] = table
    t_recv[tile] = table

    def send(phase, to_peer, to_below, to_above):
        copies = []
        for j, peer in reversed(list(enumerate(peers))):
            src, dst = to_peer
            copies.append(
                pltpu.make_async_remote_copy(
                    src, dst, send_sem.at[phase, j], recv_sem.at[phase, tile],
                    device_id=(face, peer), device_id_type=MESH,
                )
            )
        for j, (src, dst), other, slot in (
            (group - 1, to_below, below, group + 1),
            (group, to_above, above, group),
        ):
            copies.append(
                pltpu.make_async_remote_copy(
                    src, dst, send_sem.at[phase, j], recv_sem.at[phase, slot],
                    device_id=(other, tile), device_id_type=MESH,
                )
            )
        for copy in copies:
            copy.start()
        return copies

    def receive(phase, from_peer, from_below, from_above):
        for j, peer in enumerate(peers):
            ref = from_peer(peer)
            pltpu.make_async_remote_copy(
                ref, ref, send_sem.at[phase, j], recv_sem.at[phase, peer],
                device_id=(face, peer), device_id_type=MESH,
            ).wait_recv()
        for ref, slot, other in ((from_below, group, below), (from_above, group + 1, above)):
            pltpu.make_async_remote_copy(
                ref, ref, send_sem.at[phase, group], recv_sem.at[phase, slot],
                device_id=(other, tile), device_id_type=MESH,
            ).wait_recv()

    loads[1].wait()
    loads[0].wait()
    for r in blocks:
        deep = jnp.where(is_wet, lev[r : r + ROWS, :], 0)
        masks = [(deep > l).astype(F32) for l in range(2)]
        planes = []
        for l in range(2):
            mask[l, r : r + ROWS, :] = masks[l]
        for p in range(8):
            x = st[p // 2, p % 2, r : r + ROWS, :] * masks[p % 2]
            x0p[p, TOP + r : TOP + r + ROWS, :] = x
            planes.append(x)
        picked = pick_columns(planes)
        wide = iota(picked.shape, 1)
        for l in range(2):
            picked = jnp.where(wide == 16 + l, pltpu.roll(masks[l], 16 + l, 1), picked)
            picked = jnp.where(wide == 18 + l, pltpu.roll(masks[l], 19 + l, 1), picked)
        cols[0, r : r + ROWS, :] = picked

    def even_odd(even, odd):
        return jnp.where(
            lax.rem(row, 2) == 0, jnp.broadcast_to(even, (8, 128)), jnp.broadcast_to(odd, (8, 128))
        )

    def rows_of(ref, at):
        return jnp.concatenate([ref[p, at : at + 1, :] for p in range(8)], axis=0)

    turned = jnp.transpose(cols[0])
    x0 = [turned[0:8], turned[8:16], rows_of(x0p, TOP), rows_of(x0p, TOP + 127)]
    rim_mask = [
        even_odd(turned[16:17], turned[17:18]),
        even_odd(turned[18:19], turned[19:20]),
        even_odd(mask[0, 0:1, :], mask[1, 0:1, :]),
        even_odd(mask[0, 127:128, :], mask[1, 127:128, :]),
    ]
    for k in range(4):
        a_send[k] = x0[k]
        a_recv[tile, k] = x0[k]
    pl.semaphore_wait(barrier, group + 1)
    copies = send(
        0, (a_send, a_recv.at[tile]), (a_send, a_recv.at[group + 1]), (a_send, a_recv.at[group])
    )
    copies += send(
        1, (t_send, t_recv.at[tile]), (t_send, t_recv.at[group + 1]), (t_send, t_recv.at[group])
    )

    loads[2].wait()
    for r in blocks:
        planes = []
        for p in range(8):
            m = ctv[p // 2, p % 2, r : r + ROWS, :] * mask[p % 2, r : r + ROWS, :]
            m2p[p, TOP + r : TOP + r + ROWS, :] = m
            if p % 2 == 0:
                fgv[1, p // 2, r : r + ROWS, :] = m
            planes.append(m)
        cols[1, r : r + ROWS, :] = pick_columns(planes)
    fg_second = pltpu.make_async_copy(fgv.at[1], fg_out.at[0, 1], out_sem.at[0])
    fg_second.start()
    loads[3].wait()
    for r in blocks:
        planes = step_block(x0p, drive, mask, r)
        for p in range(8):
            x1p[p, TOP + r : TOP + r + ROWS, :] = planes[p]
        cols[2, r : r + ROWS, :] = pick_columns(planes)
    turned = jnp.transpose(cols[1])
    m2 = [turned[0:8], turned[8:16], rows_of(m2p, TOP), rows_of(m2p, TOP + 127)]
    turned = jnp.transpose(cols[2])
    x1 = [turned[0:8], turned[8:16], rows_of(x1p, TOP), rows_of(x1p, TOP + 127)]

    receive(0, lambda t: a_recv.at[t], a_recv.at[group], a_recv.at[group + 1])
    place = [group, group + 1, source_tile[SOUTH], source_tile[NORTH]]

    def usable(x, k):
        return x if k < 2 else jnp.where(valid[k], x, 0.0)

    halo0 = [usable(turn(a_recv[place[k], side_of[k]], k), k) for k in range(4)]
    fix1 = [rim_mask[k] * rim_step(halo0[k], x0[k], k) for k in range(4)]
    more = crossed(fix1)
    x1 = [x1[k] + more[k] for k in range(4)]
    back2 = [turn(rim_gradient(m2[k], x1[k], k), k) for k in range(4)]
    pairs = [
        jnp.where(row < 4, x1[WEST], up(x1[EAST], 4)),
        jnp.where(row < 4, x1[SOUTH], up(x1[NORTH], 4)),
    ]
    for i, value in enumerate(pairs + [back2[SOUTH], back2[NORTH]]):
        bg_send[i] = value
        bg_recv[tile, i] = value
    for i, value in enumerate(pairs + [back2[WEST]]):
        bl_send[i] = value
    for i, value in enumerate(pairs + [back2[EAST]]):
        bu_send[i] = value
    copies += send(2, (bg_send, bg_recv.at[tile]), (bl_send, bf_recv.at[1]), (bu_send, bf_recv.at[0]))

    def put_rims(fix, index, add):
        tall = jnp.concatenate([fix[WEST], fix[EAST], jnp.zeros((112, 128), F32)], axis=0)
        cols[index] = jnp.transpose(tall)
        for p in range(8):
            add(p, 0, 1, fix[SOUTH][p : p + 1])
            add(p, 127, 1, fix[NORTH][p : p + 1])

    def add_x1(p, r, n, value):
        x1p[p, TOP + r : TOP + r + n, :] = x1p[p, TOP + r : TOP + r + n, :] + value

    put_rims(fix1, 3, add_x1)
    for r in blocks:
        columns = cols[3, r : r + ROWS, :]
        for p in range(8):
            add_x1(p, r, ROWS, put_columns(columns, p))
    for r in blocks:
        planes = back_block(x1p, m2p, r)
        for p in range(8):
            part[p, r : r + ROWS, :] = planes[p]
        cols[4, r : r + ROWS, :] = pick_columns(planes)
    turned = jnp.transpose(cols[4])
    g1 = [turned[0:8], turned[8:16], rows_of(part, 0), rows_of(part, 127)]

    receive(1, lambda t: t_recv.at[t], t_recv.at[group], t_recv.at[group + 1])
    receive(2, lambda t: bg_recv.at[t], bf_recv.at[0], bf_recv.at[1])

    def pair(ref, at, k):
        both = ref[at, lax.div(side_of[k], 2)]
        return jnp.where(lax.rem(side_of[k], 2) == 1, up(both, 4), both)

    halo1 = [
        pair(bf_recv, 0, WEST), pair(bf_recv, 1, EAST),
        pair(bg_recv, source_tile[SOUTH], SOUTH), pair(bg_recv, source_tile[NORTH], NORTH),
    ]
    halo1 = [usable(turn(halo1[k], k), k) for k in range(4)]

    senders = [(t, k) for t in range(group) for k in (SOUTH, NORTH)] + [(group, EAST), (group + 1, WEST)]
    codes = [jnp.broadcast_to(t_recv[t, k : k + 1, :], (8, 128)) for t, k in senders]

    def returned(values, k):
        total = jnp.zeros((8, 128), F32)
        for seen, value in zip(codes, values):
            total = total + jnp.where(seen == me * 4 + k, value, 0.0)
        return total

    values = [bg_recv[t, k] for t in range(group) for k in (2, 3)] + [bf_recv[0, 2], bf_recv[1, 2]]
    fix2 = [rim_velocity(m2[k], halo1[k], k) + returned(values, k) for k in range(4)]
    more = crossed(fix2)
    m1 = [rim_mask[k] * (g1[k] + more[k]) for k in range(4)]
    back1 = [turn(rim_gradient(m1[k], x0[k], k), k) for k in range(4)]
    for i, k in enumerate((SOUTH, NORTH)):
        dg_send[i] = back1[k]
        dg_recv[tile, i] = back1[k]
    dl_send[0] = back1[WEST]
    du_send[0] = back1[EAST]
    copies += send(3, (dg_send, dg_recv.at[tile]), (dl_send, df_recv.at[1]), (du_send, df_recv.at[0]))

    def add_part(p, r, n, value):
        part[p, r : r + n, :] = part[p, r : r + n, :] + value

    put_rims(fix2, 5, add_part)
    for r in blocks:
        columns = cols[5, r : r + ROWS, :]
        for p in range(8):
            m = part[p, r : r + ROWS, :] + put_columns(columns, p)
            m = m * mask[p % 2, r : r + ROWS, :]
            m1p[p, TOP + r : TOP + r + ROWS, :] = m
            if p % 2 == 0:
                fgv[0, p // 2, r : r + ROWS, :] = m
    fg_first = pltpu.make_async_copy(fgv.at[0], fg_out.at[0, 0], out_sem.at[1])
    fg_first.start()
    for r in blocks:
        planes = back_block(x0p, m1p, r)
        for p in range(8):
            part[p, r : r + ROWS, :] = planes[p] * mask[p % 2, r : r + ROWS, :]
    own = [rim_velocity(m1[k], halo0[k], k) for k in range(4)]

    receive(3, lambda t: dg_recv.at[t], df_recv.at[0], df_recv.at[1])
    values = [dg_recv[t, i] for t in range(group) for i in (0, 1)] + [df_recv[0, 0], df_recv[1, 0]]
    fix3 = [rim_mask[k] * (own[k] + returned(values, k)) for k in range(4)]
    put_rims(fix3, 6, add_part)
    for r in blocks:
        columns = cols[6, r : r + ROWS, :]
        for p in range(8):
            sgv[p // 2, p % 2, r : r + ROWS, :] = part[p, r : r + ROWS, :] + put_columns(columns, p)
    sg_copy = pltpu.make_async_copy(sgv, sg_out.at[0], out_sem.at[2])
    sg_copy.start()
    for copy in copies:
        copy.wait_send()
    fg_second.wait()
    fg_first.wait()
    sg_copy.wait()


CUTS = 4


def hand_over(sg, fg, sg_out, fg_out, sem):
    copies = []
    for i, (src, dst) in enumerate(((sg, sg_out), (fg, fg_out))):
        outer, inner = src.shape[1], src.shape[2]
        for j in range(CUTS):
            piece = (0, j * outer // CUTS, pl.ds(j * outer % CUTS * inner // CUTS, outer * inner // CUTS))
            copies.append(pltpu.make_async_copy(src.at[piece], dst.at[piece], sem.at[i, j]))
    for copy in copies:
        copy.start()
    for copy in copies:
        copy.wait()


def shards(state, forcing, cotangent, neighbour, rotation, wet, levels):
    group = lax.axis_size("tile")
    anywhere = pl.BlockSpec(memory_space=pl.ANY)
    scalars = pl.BlockSpec(memory_space=pltpu.SMEM)
    fields, depth, side = state.shape[1], state.shape[2], state.shape[3]
    vm = lambda *shape: pltpu.VMEM(shape, F32)
    whole = lambda *shape: pltpu.VMEM(shape, jnp.int32)
    padded = vm(8, side + 2 * TOP, side)
    results = pl.pallas_call(
        kernel,
        out_shape=(
            jax.ShapeDtypeStruct(state.shape, F32),
            jax.ShapeDtypeStruct(forcing.shape, F32),
        ),
        in_specs=[scalars] * 3 + [anywhere] * 4,
        out_specs=(anywhere, anywhere),
        scratch_shapes=[
            vm(fields, depth, side, side), vm(fields, side, side), vm(fields, depth, side, side),
            whole(side, side), vm(depth, side, side),
            padded, padded, padded, padded,
            vm(8, side, side), vm(fields, depth, side, side), vm(2, fields, side, side),
            vm(7, side, side),
            vm(4, 8, side), vm(group + 2, 4, 8, side),
            whole(8, side), whole(group + 2, 8, side),
            vm(4, 8, side), vm(3, 8, side), vm(3, 8, side), vm(group, 4, 8, side), vm(2, 3, 8, side),
            vm(2, 8, side), vm(1, 8, side), vm(1, 8, side), vm(group, 2, 8, side), vm(2, 1, 8, side),
            pltpu.SemaphoreType.DMA((4,)), pltpu.SemaphoreType.DMA((3,)),
            pltpu.SemaphoreType.DMA((4, group + 1)), pltpu.SemaphoreType.DMA((4, group + 2)),
        ],
        compiler_params=pltpu.CompilerParams(
            collective_id=0, has_side_effects=True, vmem_limit_bytes=60 * 1024 * 1024
        ),
        name="window",
    )(neighbour, rotation, wet, state, forcing, cotangent, levels)
    return pl.pallas_call(
        hand_over,
        out_shape=tuple(jax.ShapeDtypeStruct(x.shape, F32) for x in results),
        in_specs=[anywhere] * 2,
        out_specs=(anywhere, anywhere),
        scratch_shapes=[pltpu.SemaphoreType.DMA((2, CUTS))],
        compiler_params=pltpu.CompilerParams(vmem_limit_bytes=60 * 1024 * 1024),
        name="hand_over",
    )(*results)


def solution(mesh):
    placed = (
        P(("face", "tile"), None, None, None, None),
        P(("face", "tile"), None, None, None, None),
        P(("face", "tile"), None, None, None, None),
        P(("face", "tile"), None),
        P(("face", "tile"), None),
        P(("face", "tile")),
        P(("face", "tile"), None, None),
    )
    return jax.shard_map(
        shards,
        mesh=mesh,
        in_specs=placed,
        out_specs=(
            P(("face", "tile"), None, None, None, None),
            P(("face", "tile"), None, None, None, None),
        ),
        check_vma=False,
    )
```

```python
import jax
import jax.numpy as jnp
from jax import lax
from jax.experimental import pallas as pl
from jax.experimental.pallas import tpu as pltpu
from jax.sharding import PartitionSpec as P

MESH = pl.DeviceIdType.MESH
WEST, EAST, SOUTH, NORTH = 0, 1, 2, 3
SIGN = (-1.0, 1.0, -1.0, 1.0)
TOP = 8
ROWS = 32
F32 = jnp.float32


def iota(shape, axis):
    return lax.broadcasted_iota(jnp.int32, shape, axis)


def up(x, n):
    return pltpu.roll(x, (-n) % 8, 0)


def lift(x, side):
    row = iota((8, 128), 0)
    near, far = (2, 4) if side < 2 else (4, 6)
    return jnp.where(row < 2, up(x, far), jnp.where(row < 4, up(x, near), 0.0))


def lower(theta, salt, side):
    row = iota((8, 128), 0)
    first = 4 if side < 2 else 6
    here = (row >= first) & (row < first + 2)
    return jnp.where(here, up(theta, -first) + up(salt, 2 - first), 0.0)


def rim_gradient(m, x, side):
    row = iota((8, 128), 0)
    weight = jnp.where(row < 2, 0.125, -0.1)
    return m * (0.15 - 0.5 * SIGN[side] * lift(x, side)) + SIGN[side] * weight * lift(m, side)


def rim_step(halo, x, side):
    pressure = lower(0.125 * halo, -0.1 * halo, side)
    return halo * (0.15 - 0.5 * SIGN[side] * lift(x, side)) + SIGN[side] * pressure


def rim_velocity(m, halo, side):
    product = m * halo
    return -0.5 * SIGN[side] * lower(product, product, side)


def crossed(c):
    lane = iota((8, 128), 1)
    first, last = lane == 0, lane == 127

    def at(low, high):
        return jnp.where(first, low, jnp.where(last, high, 0.0))

    right = [pltpu.roll(v, 1, 1) for v in c]
    left = [pltpu.roll(v, 127, 1) for v in c]
    return [
        c[WEST] + at(c[SOUTH], left[NORTH]),
        c[EAST] + at(right[SOUTH], c[NORTH]),
        c[SOUTH] + at(c[WEST], left[EAST]),
        c[NORTH] + at(right[WEST], c[EAST]),
    ]


def from_west(x):
    return jnp.where(iota(x.shape, 1) == 0, 0.0, pltpu.roll(x, 1, 1))


def from_east(x):
    return jnp.where(iota(x.shape, 1) == 127, 0.0, pltpu.roll(x, 127, 1))


def pick_columns(planes):
    lane = iota(planes[0].shape, 1)
    out = jnp.zeros_like(planes[0])
    for p, x in enumerate(planes):
        out = jnp.where(lane == p, pltpu.roll(x, p, 1) if p else x, out)
        out = jnp.where(lane == 8 + p, pltpu.roll(x, 9 + p, 1), out)
    return out


def put_columns(columns, p):
    lane = iota(columns.shape, 1)
    west = pltpu.roll(columns, 128 - p, 1) if p else columns
    east = pltpu.roll(columns, 119 - p, 1)
    return jnp.where(lane == 0, west, jnp.where(lane == 127, east, 0.0))


def step_block(xp, drive, mask, r):
    def at(p, shift=0):
        return xp[p, TOP + r + shift : TOP + r + shift + ROWS, :]

    out = [None] * 8
    for l in range(2):
        c = [at(2 * f + l) for f in range(4)]
        other = [at(2 * f + 1 - l) for f in range(2)]
        new = []
        grads = []
        for f in range(4):
            e, w = from_east(c[f]), from_west(c[f])
            n, s = at(2 * f + l, 1), at(2 * f + l, -1)
            lap = e + w + n + s - 4.0 * c[f]
            grads.append((0.5 * (e - w), 0.5 * (n - s)))
            new.append(c[f] + 0.15 * lap)
        u, v = c[2], c[3]
        for f in range(2):
            new[f] = new[f] - (u * grads[f][0] + v * grads[f][1]) + 0.1 * (other[f] - c[f])
        new[2] = new[2] + 0.3 * v - 0.25 * (0.8 * grads[1][0] - grads[0][0]) - 0.05 * u
        new[3] = new[3] - 0.3 * u - 0.25 * (0.8 * grads[1][1] - grads[0][1]) - 0.05 * v
        for f in range(4):
            if l == 0:
                new[f] = new[f] + drive[f, r : r + ROWS, :]
            out[2 * f + l] = new[f] * mask[l, r : r + ROWS, :]
    return out


def back_block(xp, mp, r):
    def x_at(p, shift=0):
        return xp[p, TOP + r + shift : TOP + r + shift + ROWS, :]

    def m_at(p, shift=0):
        return mp[p, TOP + r + shift : TOP + r + shift + ROWS, :]

    out = [None] * 8
    for l in range(2):
        u = 0.5 * x_at(4 + l)
        v_s, v_n = 0.5 * x_at(6 + l, -1), 0.5 * x_at(6 + l, 1)
        c, d = m_at(4 + l), m_at(6 + l)
        c_s, c_n, d_s, d_n = m_at(4 + l, -1), m_at(4 + l, 1), m_at(6 + l, -1), m_at(6 + l, 1)
        g_u = 0.15 * (from_west(c) + from_east(c) + c_s + c_n) + 0.35 * c - 0.3 * d
        g_v = 0.15 * (from_west(d) + from_east(d) + d_s + d_n) + 0.35 * d + 0.3 * c
        for f, k in ((0, 0.125), (1, -0.1)):
            p = 2 * f + l
            a, a_s, a_n, a_o = m_at(p), m_at(p, -1), m_at(p, 1), m_at(2 * f + 1 - l)
            kc = k * c
            au = a * u
            a15 = 0.15 * a
            g = from_west(a15 - au + kc) + from_east(a15 + au - kc)
            g = g + a_s * (0.15 - v_s) + a_n * (0.15 + v_n) + k * (d_s - d_n)
            out[p] = g + 0.3 * a + 0.1 * a_o
            x = x_at(p)
            half = 0.5 * a
            g_u = g_u - half * (from_east(x) - from_west(x))
            g_v = g_v - half * (x_at(p, 1) - x_at(p, -1))
        out[4 + l], out[6 + l] = g_u, g_v
    return out


def kernel(
    nb, rot, wet, state, forcing, cot, levels, sg_out, fg_out,
    st, drive, ctv, lev, mask, x0p, x1p, m2p, m1p, part, sgv, fgv, cols,
    a_send, a_recv, t_send, t_recv,
    bg_send, bl_send, bu_send, bg_recv, bf_recv,
    dg_send, dl_send, du_send, dg_recv, df_recv,
    in_sem, out_sem, send_sem, recv_sem,
):
    group, faces = lax.axis_size("tile"), lax.axis_size("face")
    face, tile = lax.axis_index("face"), lax.axis_index("tile")
    below, above = lax.rem(face + faces - 1, faces), lax.rem(face + 1, faces)
    peers = [lax.rem(tile + j, group) for j in range(1, group)]
    me = face * group + tile
    blocks = range(0, 128, ROWS)

    loads = [
        pltpu.make_async_copy(state.at[0], st, in_sem.at[0]),
        pltpu.make_async_copy(levels.at[0], lev, in_sem.at[1]),
        pltpu.make_async_copy(cot.at[0], ctv, in_sem.at[2]),
        pltpu.make_async_copy(forcing.at[0, 0], drive, in_sem.at[3]),
    ]
    for load in loads:
        load.start()
    barrier = pltpu.get_barrier_semaphore()
    for peer in peers:
        pl.semaphore_signal(barrier, inc=1, device_id=(face, peer), device_id_type=MESH)
    for other in (below, above):
        pl.semaphore_signal(barrier, inc=1, device_id=(other, tile), device_id_type=MESH)

    pad = jnp.zeros((8, TOP, 128), F32)
    for ref in (x0p, x1p, m2p, m1p):
        ref[:, 0:TOP, :] = pad
        ref[:, TOP + 128 : 2 * TOP + 128, :] = pad

    side_of = [lax.rem(rot[0, k], 4) for k in range(4)]
    flip = [rot[0, k] >= 4 for k in range(4)]
    source = [nb[0, k] for k in range(4)]
    valid = [s >= 0 for s in source]
    source_tile = [lax.rem(jnp.maximum(s, 0), group) for s in source]
    code = [jnp.where(valid[k], source[k] * 4 + side_of[k], -1) for k in range(4)]
    is_wet = wet[0] == 1
    lane = iota((8, 128), 1)
    row = iota((8, 128), 0)

    def turn(x, k):
        back = jnp.take_along_axis(x, 127 - lane, axis=1)
        return jnp.where(flip[k], back, x)

    table = jnp.full((8, 128), -1, jnp.int32)
    for k in range(4):
        table = jnp.where(row == k, code[k], table)
    t_send[...] = table
    t_recv[tile] = table

    def send(phase, to_peer, to_below, to_above):
        copies = []
        for j, peer in reversed(list(enumerate(peers))):
            src, dst = to_peer
            copies.append(
                pltpu.make_async_remote_copy(
                    src, dst, send_sem.at[phase, j], recv_sem.at[phase, tile],
                    device_id=(face, peer), device_id_type=MESH,
                )
            )
        for j, (src, dst), other, slot in (
            (group - 1, to_below, below, group + 1),
            (group, to_above, above, group),
        ):
            copies.append(
                pltpu.make_async_remote_copy(
                    src, dst, send_sem.at[phase, j], recv_sem.at[phase, slot],
                    device_id=(other, tile), device_id_type=MESH,
                )
            )
        for copy in copies:
            copy.start()
        return copies

    def receive(phase, from_peer, from_below, from_above):
        for j, peer in enumerate(peers):
            ref = from_peer(peer)
            pltpu.make_async_remote_copy(
                ref, ref, send_sem.at[phase, j], recv_sem.at[phase, peer],
                device_id=(face, peer), device_id_type=MESH,
            ).wait_recv()
        for ref, slot, other in ((from_below, group, below), (from_above, group + 1, above)):
            pltpu.make_async_remote_copy(
                ref, ref, send_sem.at[phase, group], recv_sem.at[phase, slot],
                device_id=(other, tile), device_id_type=MESH,
            ).wait_recv()

    loads[1].wait()
    loads[0].wait()
    for r in blocks:
        deep = jnp.where(is_wet, lev[r : r + ROWS, :], 0)
        masks = [(deep > l).astype(F32) for l in range(2)]
        planes = []
        for l in range(2):
            mask[l, r : r + ROWS, :] = masks[l]
        for p in range(8):
            x = st[p // 2, p % 2, r : r + ROWS, :] * masks[p % 2]
            x0p[p, TOP + r : TOP + r + ROWS, :] = x
            planes.append(x)
        picked = pick_columns(planes)
        wide = iota(picked.shape, 1)
        for l in range(2):
            picked = jnp.where(wide == 16 + l, pltpu.roll(masks[l], 16 + l, 1), picked)
            picked = jnp.where(wide == 18 + l, pltpu.roll(masks[l], 19 + l, 1), picked)
        cols[0, r : r + ROWS, :] = picked

    def even_odd(even, odd):
        return jnp.where(
            lax.rem(row, 2) == 0, jnp.broadcast_to(even, (8, 128)), jnp.broadcast_to(odd, (8, 128))
        )

    def rows_of(ref, at):
        return jnp.concatenate([ref[p, at : at + 1, :] for p in range(8)], axis=0)

    turned = jnp.transpose(cols[0])
    x0 = [turned[0:8], turned[8:16], rows_of(x0p, TOP), rows_of(x0p, TOP + 127)]
    rim_mask = [
        even_odd(turned[16:17], turned[17:18]),
        even_odd(turned[18:19], turned[19:20]),
        even_odd(mask[0, 0:1, :], mask[1, 0:1, :]),
        even_odd(mask[0, 127:128, :], mask[1, 127:128, :]),
    ]
    for k in range(4):
        a_send[k] = x0[k]
        a_recv[tile, k] = x0[k]
    pl.semaphore_wait(barrier, group + 1)
    copies = send(
        0, (a_send, a_recv.at[tile]), (a_send, a_recv.at[group + 1]), (a_send, a_recv.at[group])
    )
    copies += send(
        1, (t_send, t_recv.at[tile]), (t_send, t_recv.at[group + 1]), (t_send, t_recv.at[group])
    )

    loads[2].wait()
    for r in blocks:
        planes = []
        for p in range(8):
            m = ctv[p // 2, p % 2, r : r + ROWS, :] * mask[p % 2, r : r + ROWS, :]
            m2p[p, TOP + r : TOP + r + ROWS, :] = m
            if p % 2 == 0:
                fgv[1, p // 2, r : r + ROWS, :] = m
            planes.append(m)
        cols[1, r : r + ROWS, :] = pick_columns(planes)
    fg_second = pltpu.make_async_copy(fgv.at[1], fg_out.at[0, 1], out_sem.at[0])
    fg_second.start()
    loads[3].wait()
    for r in blocks:
        planes = step_block(x0p, drive, mask, r)
        for p in range(8):
            x1p[p, TOP + r : TOP + r + ROWS, :] = planes[p]
        cols[2, r : r + ROWS, :] = pick_columns(planes)
    turned = jnp.transpose(cols[1])
    m2 = [turned[0:8], turned[8:16], rows_of(m2p, TOP), rows_of(m2p, TOP + 127)]
    turned = jnp.transpose(cols[2])
    x1 = [turned[0:8], turned[8:16], rows_of(x1p, TOP), rows_of(x1p, TOP + 127)]

    receive(0, lambda t: a_recv.at[t], a_recv.at[group], a_recv.at[group + 1])
    place = [group, group + 1, source_tile[SOUTH], source_tile[NORTH]]

    def usable(x, k):
        return x if k < 2 else jnp.where(valid[k], x, 0.0)

    halo0 = [usable(turn(a_recv[place[k], side_of[k]], k), k) for k in range(4)]
    fix1 = [rim_mask[k] * rim_step(halo0[k], x0[k], k) for k in range(4)]
    more = crossed(fix1)
    x1 = [x1[k] + more[k] for k in range(4)]
    back2 = [turn(rim_gradient(m2[k], x1[k], k), k) for k in range(4)]
    pairs = [
        jnp.where(row < 4, x1[WEST], up(x1[EAST], 4)),
        jnp.where(row < 4, x1[SOUTH], up(x1[NORTH], 4)),
    ]
    for i, value in enumerate(pairs + [back2[SOUTH], back2[NORTH]]):
        bg_send[i] = value
        bg_recv[tile, i] = value
    for i, value in enumerate(pairs + [back2[WEST]]):
        bl_send[i] = value
    for i, value in enumerate(pairs + [back2[EAST]]):
        bu_send[i] = value
    copies += send(2, (bg_send, bg_recv.at[tile]), (bl_send, bf_recv.at[1]), (bu_send, bf_recv.at[0]))

    def put_rims(fix, index, add):
        tall = jnp.concatenate([fix[WEST], fix[EAST], jnp.zeros((112, 128), F32)], axis=0)
        cols[index] = jnp.transpose(tall)
        for p in range(8):
            add(p, 0, 1, fix[SOUTH][p : p + 1])
            add(p, 127, 1, fix[NORTH][p : p + 1])

    def add_x1(p, r, n, value):
        x1p[p, TOP + r : TOP + r + n, :] = x1p[p, TOP + r : TOP + r + n, :] + value

    put_rims(fix1, 3, add_x1)
    for r in blocks:
        columns = cols[3, r : r + ROWS, :]
        for p in range(8):
            add_x1(p, r, ROWS, put_columns(columns, p))
    for r in blocks:
        planes = back_block(x1p, m2p, r)
        for p in range(8):
            part[p, r : r + ROWS, :] = planes[p]
        cols[4, r : r + ROWS, :] = pick_columns(planes)
    turned = jnp.transpose(cols[4])
    g1 = [turned[0:8], turned[8:16], rows_of(part, 0), rows_of(part, 127)]

    receive(1, lambda t: t_recv.at[t], t_recv.at[group], t_recv.at[group + 1])
    receive(2, lambda t: bg_recv.at[t], bf_recv.at[0], bf_recv.at[1])

    def pair(ref, at, k):
        both = ref[at, lax.div(side_of[k], 2)]
        return jnp.where(lax.rem(side_of[k], 2) == 1, up(both, 4), both)

    halo1 = [
        pair(bf_recv, 0, WEST), pair(bf_recv, 1, EAST),
        pair(bg_recv, source_tile[SOUTH], SOUTH), pair(bg_recv, source_tile[NORTH], NORTH),
    ]
    halo1 = [usable(turn(halo1[k], k), k) for k in range(4)]

    senders = [(t, k) for t in range(group) for k in (SOUTH, NORTH)] + [(group, EAST), (group + 1, WEST)]
    codes = [jnp.broadcast_to(t_recv[t, k : k + 1, :], (8, 128)) for t, k in senders]

    def returned(values, k):
        total = jnp.zeros((8, 128), F32)
        for seen, value in zip(codes, values):
            total = total + jnp.where(seen == me * 4 + k, value, 0.0)
        return total

    values = [bg_recv[t, k] for t in range(group) for k in (2, 3)] + [bf_recv[0, 2], bf_recv[1, 2]]
    fix2 = [rim_velocity(m2[k], halo1[k], k) + returned(values, k) for k in range(4)]
    more = crossed(fix2)
    m1 = [rim_mask[k] * (g1[k] + more[k]) for k in range(4)]
    back1 = [turn(rim_gradient(m1[k], x0[k], k), k) for k in range(4)]
    for i, k in enumerate((SOUTH, NORTH)):
        dg_send[i] = back1[k]
        dg_recv[tile, i] = back1[k]
    dl_send[0] = back1[WEST]
    du_send[0] = back1[EAST]
    copies += send(3, (dg_send, dg_recv.at[tile]), (dl_send, df_recv.at[1]), (du_send, df_recv.at[0]))

    def add_part(p, r, n, value):
        part[p, r : r + n, :] = part[p, r : r + n, :] + value

    put_rims(fix2, 5, add_part)
    for r in blocks:
        columns = cols[5, r : r + ROWS, :]
        for p in range(8):
            m = part[p, r : r + ROWS, :] + put_columns(columns, p)
            m = m * mask[p % 2, r : r + ROWS, :]
            m1p[p, TOP + r : TOP + r + ROWS, :] = m
            if p % 2 == 0:
                fgv[0, p // 2, r : r + ROWS, :] = m
    fg_first = pltpu.make_async_copy(fgv.at[0], fg_out.at[0, 0], out_sem.at[1])
    fg_first.start()
    for r in blocks:
        planes = back_block(x0p, m1p, r)
        for p in range(8):
            part[p, r : r + ROWS, :] = planes[p] * mask[p % 2, r : r + ROWS, :]
    own = [rim_velocity(m1[k], halo0[k], k) for k in range(4)]

    receive(3, lambda t: dg_recv.at[t], df_recv.at[0], df_recv.at[1])
    values = [dg_recv[t, i] for t in range(group) for i in (0, 1)] + [df_recv[0, 0], df_recv[1, 0]]
    fix3 = [rim_mask[k] * (own[k] + returned(values, k)) for k in range(4)]
    put_rims(fix3, 6, add_part)
    for r in blocks:
        columns = cols[6, r : r + ROWS, :]
        for p in range(8):
            sgv[p // 2, p % 2, r : r + ROWS, :] = part[p, r : r + ROWS, :] + put_columns(columns, p)
    sg_copy = pltpu.make_async_copy(sgv, sg_out.at[0], out_sem.at[2])
    sg_copy.start()
    for copy in copies:
        copy.wait_send()
    fg_second.wait()
    fg_first.wait()
    sg_copy.wait()


CUTS = 4


def hand_over(sg, fg, sg_out, fg_out, held, load_sem, store_sem):
    loads, stores = [], []
    for i, (src, dst) in enumerate(((sg, sg_out), (fg, fg_out))):
        outer, inner = src.shape[1], src.shape[2]
        for j in range(CUTS):
            piece = (0, j * outer // CUTS, pl.ds(j * outer % CUTS * inner // CUTS, outer * inner // CUTS))
            loads.append(pltpu.make_async_copy(src.at[piece], held.at[i, j], load_sem.at[i, j]))
            stores.append(pltpu.make_async_copy(held.at[i, j], dst.at[piece], store_sem.at[i, j]))
    for load in loads:
        load.start()
    for load, store in zip(loads, stores):
        load.wait()
        store.start()
    for store in stores:
        store.wait()


def shards(state, forcing, cotangent, neighbour, rotation, wet, levels):
    group = lax.axis_size("tile")
    anywhere = pl.BlockSpec(memory_space=pl.ANY)
    scalars = pl.BlockSpec(memory_space=pltpu.SMEM)
    fields, depth, side = state.shape[1], state.shape[2], state.shape[3]
    vm = lambda *shape: pltpu.VMEM(shape, F32)
    whole = lambda *shape: pltpu.VMEM(shape, jnp.int32)
    padded = vm(8, side + 2 * TOP, side)
    results = pl.pallas_call(
        kernel,
        out_shape=(
            jax.ShapeDtypeStruct(state.shape, F32),
            jax.ShapeDtypeStruct(forcing.shape, F32),
        ),
        in_specs=[scalars] * 3 + [anywhere] * 4,
        out_specs=(anywhere, anywhere),
        scratch_shapes=[
            vm(fields, depth, side, side), vm(fields, side, side), vm(fields, depth, side, side),
            whole(side, side), vm(depth, side, side),
            padded, padded, padded, padded,
            vm(8, side, side), vm(fields, depth, side, side), vm(2, fields, side, side),
            vm(7, side, side),
            vm(4, 8, side), vm(group + 2, 4, 8, side),
            whole(8, side), whole(group + 2, 8, side),
            vm(4, 8, side), vm(3, 8, side), vm(3, 8, side), vm(group, 4, 8, side), vm(2, 3, 8, side),
            vm(2, 8, side), vm(1, 8, side), vm(1, 8, side), vm(group, 2, 8, side), vm(2, 1, 8, side),
            pltpu.SemaphoreType.DMA((4,)), pltpu.SemaphoreType.DMA((3,)),
            pltpu.SemaphoreType.DMA((4, group + 1)), pltpu.SemaphoreType.DMA((4, group + 2)),
        ],
        compiler_params=pltpu.CompilerParams(
            collective_id=0, has_side_effects=True, vmem_limit_bytes=60 * 1024 * 1024
        ),
        name="window",
    )(neighbour, rotation, wet, state, forcing, cotangent, levels)
    return pl.pallas_call(
        hand_over,
        out_shape=tuple(jax.ShapeDtypeStruct(x.shape, F32) for x in results),
        in_specs=[anywhere] * 2,
        out_specs=(anywhere, anywhere),
        scratch_shapes=[
            vm(2, CUTS, fields * depth // CUTS, side, side),
            pltpu.SemaphoreType.DMA((2, CUTS)), pltpu.SemaphoreType.DMA((2, CUTS)),
        ],
        compiler_params=pltpu.CompilerParams(vmem_limit_bytes=60 * 1024 * 1024),
        name="hand_over",
    )(*results)


def solution(mesh):
    placed = (
        P(("face", "tile"), None, None, None, None),
        P(("face", "tile"), None, None, None, None),
        P(("face", "tile"), None, None, None, None),
        P(("face", "tile"), None),
        P(("face", "tile"), None),
        P(("face", "tile")),
        P(("face", "tile"), None, None),
    )
    return jax.shard_map(
        shards,
        mesh=mesh,
        in_specs=placed,
        out_specs=(
            P(("face", "tile"), None, None, None, None),
            P(("face", "tile"), None, None, None, None),
        ),
        check_vma=False,
    )
```

```python
import jax
import jax.numpy as jnp
from jax import lax
from jax.experimental import pallas as pl
from jax.experimental.pallas import tpu as pltpu
from jax.sharding import PartitionSpec as P

MESH = pl.DeviceIdType.MESH
WEST, EAST, SOUTH, NORTH = 0, 1, 2, 3
SIGN = (-1.0, 1.0, -1.0, 1.0)
TOP = 8
ROWS = 32
F32 = jnp.float32


def iota(shape, axis):
    return lax.broadcasted_iota(jnp.int32, shape, axis)


def up(x, n):
    return pltpu.roll(x, (-n) % 8, 0)


def lift(x, side):
    row = iota((8, 128), 0)
    near, far = (2, 4) if side < 2 else (4, 6)
    return jnp.where(row < 2, up(x, far), jnp.where(row < 4, up(x, near), 0.0))


def lower(theta, salt, side):
    row = iota((8, 128), 0)
    first = 4 if side < 2 else 6
    here = (row >= first) & (row < first + 2)
    return jnp.where(here, up(theta, -first) + up(salt, 2 - first), 0.0)


def rim_gradient(m, x, side):
    row = iota((8, 128), 0)
    weight = jnp.where(row < 2, 0.125, -0.1)
    return m * (0.15 - 0.5 * SIGN[side] * lift(x, side)) + SIGN[side] * weight * lift(m, side)


def rim_step(halo, x, side):
    pressure = lower(0.125 * halo, -0.1 * halo, side)
    return halo * (0.15 - 0.5 * SIGN[side] * lift(x, side)) + SIGN[side] * pressure


def rim_velocity(m, halo, side):
    product = m * halo
    return -0.5 * SIGN[side] * lower(product, product, side)


def crossed(c):
    lane = iota((8, 128), 1)
    first, last = lane == 0, lane == 127

    def at(low, high):
        return jnp.where(first, low, jnp.where(last, high, 0.0))

    right = [pltpu.roll(v, 1, 1) for v in c]
    left = [pltpu.roll(v, 127, 1) for v in c]
    return [
        c[WEST] + at(c[SOUTH], left[NORTH]),
        c[EAST] + at(right[SOUTH], c[NORTH]),
        c[SOUTH] + at(c[WEST], left[EAST]),
        c[NORTH] + at(right[WEST], c[EAST]),
    ]


def from_west(x):
    return jnp.where(iota(x.shape, 1) == 0, 0.0, pltpu.roll(x, 1, 1))


def from_east(x):
    return jnp.where(iota(x.shape, 1) == 127, 0.0, pltpu.roll(x, 127, 1))


def pick_columns(planes):
    lane = iota(planes[0].shape, 1)
    out = jnp.zeros_like(planes[0])
    for p, x in enumerate(planes):
        out = jnp.where(lane == p, pltpu.roll(x, p, 1) if p else x, out)
        out = jnp.where(lane == 8 + p, pltpu.roll(x, 9 + p, 1), out)
    return out


def put_columns(columns, p):
    lane = iota(columns.shape, 1)
    west = pltpu.roll(columns, 128 - p, 1) if p else columns
    east = pltpu.roll(columns, 119 - p, 1)
    return jnp.where(lane == 0, west, jnp.where(lane == 127, east, 0.0))


def step_block(xp, drive, mask, r):
    def at(p, shift=0):
        return xp[p, TOP + r + shift : TOP + r + shift + ROWS, :]

    out = [None] * 8
    for l in range(2):
        c = [at(2 * f + l) for f in range(4)]
        other = [at(2 * f + 1 - l) for f in range(2)]
        new = []
        grads = []
        for f in range(4):
            e, w = from_east(c[f]), from_west(c[f])
            n, s = at(2 * f + l, 1), at(2 * f + l, -1)
            lap = e + w + n + s - 4.0 * c[f]
            grads.append((0.5 * (e - w), 0.5 * (n - s)))
            new.append(c[f] + 0.15 * lap)
        u, v = c[2], c[3]
        for f in range(2):
            new[f] = new[f] - (u * grads[f][0] + v * grads[f][1]) + 0.1 * (other[f] - c[f])
        new[2] = new[2] + 0.3 * v - 0.25 * (0.8 * grads[1][0] - grads[0][0]) - 0.05 * u
        new[3] = new[3] - 0.3 * u - 0.25 * (0.8 * grads[1][1] - grads[0][1]) - 0.05 * v
        for f in range(4):
            if l == 0:
                new[f] = new[f] + drive[f, r : r + ROWS, :]
            out[2 * f + l] = new[f] * mask[l, r : r + ROWS, :]
    return out


def back_block(xp, mp, r):
    def x_at(p, shift=0):
        return xp[p, TOP + r + shift : TOP + r + shift + ROWS, :]

    def m_at(p, shift=0):
        return mp[p, TOP + r + shift : TOP + r + shift + ROWS, :]

    out = [None] * 8
    for l in range(2):
        u = 0.5 * x_at(4 + l)
        v_s, v_n = 0.5 * x_at(6 + l, -1), 0.5 * x_at(6 + l, 1)
        c, d = m_at(4 + l), m_at(6 + l)
        c_s, c_n, d_s, d_n = m_at(4 + l, -1), m_at(4 + l, 1), m_at(6 + l, -1), m_at(6 + l, 1)
        g_u = 0.15 * (from_west(c) + from_east(c) + c_s + c_n) + 0.35 * c - 0.3 * d
        g_v = 0.15 * (from_west(d) + from_east(d) + d_s + d_n) + 0.35 * d + 0.3 * c
        for f, k in ((0, 0.125), (1, -0.1)):
            p = 2 * f + l
            a, a_s, a_n, a_o = m_at(p), m_at(p, -1), m_at(p, 1), m_at(2 * f + 1 - l)
            kc = k * c
            au = a * u
            a15 = 0.15 * a
            g = from_west(a15 - au + kc) + from_east(a15 + au - kc)
            g = g + a_s * (0.15 - v_s) + a_n * (0.15 + v_n) + k * (d_s - d_n)
            out[p] = g + 0.3 * a + 0.1 * a_o
            x = x_at(p)
            half = 0.5 * a
            g_u = g_u - half * (from_east(x) - from_west(x))
            g_v = g_v - half * (x_at(p, 1) - x_at(p, -1))
        out[4 + l], out[6 + l] = g_u, g_v
    return out


def kernel(
    nb, rot, wet, state, forcing, cot, levels, sg_out, fg_out,
    st, drive, ctv, lev, mask, x0p, x1p, m2p, m1p, part, cols,
    a_send, a_recv, t_send, t_recv,
    bg_send, bl_send, bu_send, bg_recv, bf_recv,
    dg_send, dl_send, du_send, dg_recv, df_recv,
    in_sem, send_sem, recv_sem,
):
    group, faces = lax.axis_size("tile"), lax.axis_size("face")
    face, tile = lax.axis_index("face"), lax.axis_index("tile")
    below, above = lax.rem(face + faces - 1, faces), lax.rem(face + 1, faces)
    peers = [lax.rem(tile + j, group) for j in range(1, group)]
    me = face * group + tile
    blocks = range(0, 128, ROWS)

    loads = [
        pltpu.make_async_copy(state.at[0], st, in_sem.at[0]),
        pltpu.make_async_copy(levels.at[0], lev, in_sem.at[1]),
        pltpu.make_async_copy(cot.at[0], ctv, in_sem.at[2]),
        pltpu.make_async_copy(forcing.at[0, 0], drive, in_sem.at[3]),
    ]
    for load in loads:
        load.start()
    barrier = pltpu.get_barrier_semaphore()
    for peer in peers:
        pl.semaphore_signal(barrier, inc=1, device_id=(face, peer), device_id_type=MESH)
    for other in (below, above):
        pl.semaphore_signal(barrier, inc=1, device_id=(other, tile), device_id_type=MESH)

    pad = jnp.zeros((8, TOP, 128), F32)
    for ref in (x0p, x1p, m2p, m1p):
        ref[:, 0:TOP, :] = pad
        ref[:, TOP + 128 : 2 * TOP + 128, :] = pad

    side_of = [lax.rem(rot[0, k], 4) for k in range(4)]
    flip = [rot[0, k] >= 4 for k in range(4)]
    source = [nb[0, k] for k in range(4)]
    valid = [s >= 0 for s in source]
    source_tile = [lax.rem(jnp.maximum(s, 0), group) for s in source]
    code = [jnp.where(valid[k], source[k] * 4 + side_of[k], -1) for k in range(4)]
    is_wet = wet[0] == 1
    lane = iota((8, 128), 1)
    row = iota((8, 128), 0)

    def turn(x, k):
        back = jnp.take_along_axis(x, 127 - lane, axis=1)
        return jnp.where(flip[k], back, x)

    table = jnp.full((8, 128), -1, jnp.int32)
    for k in range(4):
        table = jnp.where(row == k, code[k], table)
    t_send[...] = table
    t_recv[tile] = table

    def send(phase, to_peer, to_below, to_above):
        copies = []
        for j, peer in reversed(list(enumerate(peers))):
            src, dst = to_peer
            copies.append(
                pltpu.make_async_remote_copy(
                    src, dst, send_sem.at[phase, j], recv_sem.at[phase, tile],
                    device_id=(face, peer), device_id_type=MESH,
                )
            )
        for j, (src, dst), other, slot in (
            (group - 1, to_below, below, group + 1),
            (group, to_above, above, group),
        ):
            copies.append(
                pltpu.make_async_remote_copy(
                    src, dst, send_sem.at[phase, j], recv_sem.at[phase, slot],
                    device_id=(other, tile), device_id_type=MESH,
                )
            )
        for copy in copies:
            copy.start()
        return copies

    def receive(phase, from_peer, from_below, from_above):
        for j, peer in enumerate(peers):
            ref = from_peer(peer)
            pltpu.make_async_remote_copy(
                ref, ref, send_sem.at[phase, j], recv_sem.at[phase, peer],
                device_id=(face, peer), device_id_type=MESH,
            ).wait_recv()
        for ref, slot, other in ((from_below, group, below), (from_above, group + 1, above)):
            pltpu.make_async_remote_copy(
                ref, ref, send_sem.at[phase, group], recv_sem.at[phase, slot],
                device_id=(other, tile), device_id_type=MESH,
            ).wait_recv()

    loads[1].wait()
    loads[0].wait()
    for r in blocks:
        deep = jnp.where(is_wet, lev[r : r + ROWS, :], 0)
        masks = [(deep > l).astype(F32) for l in range(2)]
        planes = []
        for l in range(2):
            mask[l, r : r + ROWS, :] = masks[l]
        for p in range(8):
            x = st[p // 2, p % 2, r : r + ROWS, :] * masks[p % 2]
            x0p[p, TOP + r : TOP + r + ROWS, :] = x
            planes.append(x)
        picked = pick_columns(planes)
        wide = iota(picked.shape, 1)
        for l in range(2):
            picked = jnp.where(wide == 16 + l, pltpu.roll(masks[l], 16 + l, 1), picked)
            picked = jnp.where(wide == 18 + l, pltpu.roll(masks[l], 19 + l, 1), picked)
        cols[0, r : r + ROWS, :] = picked

    def even_odd(even, odd):
        return jnp.where(
            lax.rem(row, 2) == 0, jnp.broadcast_to(even, (8, 128)), jnp.broadcast_to(odd, (8, 128))
        )

    def rows_of(ref, at):
        return jnp.concatenate([ref[p, at : at + 1, :] for p in range(8)], axis=0)

    turned = jnp.transpose(cols[0])
    x0 = [turned[0:8], turned[8:16], rows_of(x0p, TOP), rows_of(x0p, TOP + 127)]
    rim_mask = [
        even_odd(turned[16:17], turned[17:18]),
        even_odd(turned[18:19], turned[19:20]),
        even_odd(mask[0, 0:1, :], mask[1, 0:1, :]),
        even_odd(mask[0, 127:128, :], mask[1, 127:128, :]),
    ]
    for k in range(4):
        a_send[k] = x0[k]
        a_recv[tile, k] = x0[k]
    pl.semaphore_wait(barrier, group + 1)
    copies = send(
        0, (a_send, a_recv.at[tile]), (a_send, a_recv.at[group + 1]), (a_send, a_recv.at[group])
    )
    copies += send(
        1, (t_send, t_recv.at[tile]), (t_send, t_recv.at[group + 1]), (t_send, t_recv.at[group])
    )

    loads[2].wait()
    for r in blocks:
        planes = []
        for p in range(8):
            m = ctv[p // 2, p % 2, r : r + ROWS, :] * mask[p % 2, r : r + ROWS, :]
            m2p[p, TOP + r : TOP + r + ROWS, :] = m
            if p % 2 == 0:
                fg_out[0, 1, p // 2, r : r + ROWS, :] = m
            planes.append(m)
        cols[1, r : r + ROWS, :] = pick_columns(planes)
    loads[3].wait()
    for r in blocks:
        planes = step_block(x0p, drive, mask, r)
        for p in range(8):
            x1p[p, TOP + r : TOP + r + ROWS, :] = planes[p]
        cols[2, r : r + ROWS, :] = pick_columns(planes)
    turned = jnp.transpose(cols[1])
    m2 = [turned[0:8], turned[8:16], rows_of(m2p, TOP), rows_of(m2p, TOP + 127)]
    turned = jnp.transpose(cols[2])
    x1 = [turned[0:8], turned[8:16], rows_of(x1p, TOP), rows_of(x1p, TOP + 127)]

    receive(0, lambda t: a_recv.at[t], a_recv.at[group], a_recv.at[group + 1])
    place = [group, group + 1, source_tile[SOUTH], source_tile[NORTH]]

    def usable(x, k):
        return x if k < 2 else jnp.where(valid[k], x, 0.0)

    halo0 = [usable(turn(a_recv[place[k], side_of[k]], k), k) for k in range(4)]
    fix1 = [rim_mask[k] * rim_step(halo0[k], x0[k], k) for k in range(4)]
    more = crossed(fix1)
    x1 = [x1[k] + more[k] for k in range(4)]
    back2 = [turn(rim_gradient(m2[k], x1[k], k), k) for k in range(4)]
    pairs = [
        jnp.where(row < 4, x1[WEST], up(x1[EAST], 4)),
        jnp.where(row < 4, x1[SOUTH], up(x1[NORTH], 4)),
    ]
    for i, value in enumerate(pairs + [back2[SOUTH], back2[NORTH]]):
        bg_send[i] = value
        bg_recv[tile, i] = value
    for i, value in enumerate(pairs + [back2[WEST]]):
        bl_send[i] = value
    for i, value in enumerate(pairs + [back2[EAST]]):
        bu_send[i] = value
    copies += send(2, (bg_send, bg_recv.at[tile]), (bl_send, bf_recv.at[1]), (bu_send, bf_recv.at[0]))

    def put_rims(fix, index, add):
        tall = jnp.concatenate([fix[WEST], fix[EAST], jnp.zeros((112, 128), F32)], axis=0)
        cols[index] = jnp.transpose(tall)
        for p in range(8):
            add(p, 0, 1, fix[SOUTH][p : p + 1])
            add(p, 127, 1, fix[NORTH][p : p + 1])

    def add_x1(p, r, n, value):
        x1p[p, TOP + r : TOP + r + n, :] = x1p[p, TOP + r : TOP + r + n, :] + value

    put_rims(fix1, 3, add_x1)
    for r in blocks:
        columns = cols[3, r : r + ROWS, :]
        for p in range(8):
            add_x1(p, r, ROWS, put_columns(columns, p))
    for r in blocks:
        planes = back_block(x1p, m2p, r)
        for p in range(8):
            part[p, r : r + ROWS, :] = planes[p]
        cols[4, r : r + ROWS, :] = pick_columns(planes)
    turned = jnp.transpose(cols[4])
    g1 = [turned[0:8], turned[8:16], rows_of(part, 0), rows_of(part, 127)]

    receive(1, lambda t: t_recv.at[t], t_recv.at[group], t_recv.at[group + 1])
    receive(2, lambda t: bg_recv.at[t], bf_recv.at[0], bf_recv.at[1])

    def pair(ref, at, k):
        both = ref[at, lax.div(side_of[k], 2)]
        return jnp.where(lax.rem(side_of[k], 2) == 1, up(both, 4), both)

    halo1 = [
        pair(bf_recv, 0, WEST), pair(bf_recv, 1, EAST),
        pair(bg_recv, source_tile[SOUTH], SOUTH), pair(bg_recv, source_tile[NORTH], NORTH),
    ]
    halo1 = [usable(turn(halo1[k], k), k) for k in range(4)]

    senders = [(t, k) for t in range(group) for k in (SOUTH, NORTH)] + [(group, EAST), (group + 1, WEST)]
    codes = [jnp.broadcast_to(t_recv[t, k : k + 1, :], (8, 128)) for t, k in senders]

    def returned(values, k):
        total = jnp.zeros((8, 128), F32)
        for seen, value in zip(codes, values):
            total = total + jnp.where(seen == me * 4 + k, value, 0.0)
        return total

    values = [bg_recv[t, k] for t in range(group) for k in (2, 3)] + [bf_recv[0, 2], bf_recv[1, 2]]
    fix2 = [rim_velocity(m2[k], halo1[k], k) + returned(values, k) for k in range(4)]
    more = crossed(fix2)
    m1 = [rim_mask[k] * (g1[k] + more[k]) for k in range(4)]
    back1 = [turn(rim_gradient(m1[k], x0[k], k), k) for k in range(4)]
    for i, k in enumerate((SOUTH, NORTH)):
        dg_send[i] = back1[k]
        dg_recv[tile, i] = back1[k]
    dl_send[0] = back1[WEST]
    du_send[0] = back1[EAST]
    copies += send(3, (dg_send, dg_recv.at[tile]), (dl_send, df_recv.at[1]), (du_send, df_recv.at[0]))

    def add_part(p, r, n, value):
        part[p, r : r + n, :] = part[p, r : r + n, :] + value

    put_rims(fix2, 5, add_part)
    for r in blocks:
        columns = cols[5, r : r + ROWS, :]
        for p in range(8):
            m = part[p, r : r + ROWS, :] + put_columns(columns, p)
            m = m * mask[p % 2, r : r + ROWS, :]
            m1p[p, TOP + r : TOP + r + ROWS, :] = m
            if p % 2 == 0:
                fg_out[0, 0, p // 2, r : r + ROWS, :] = m
    for r in blocks:
        planes = back_block(x0p, m1p, r)
        for p in range(8):
            part[p, r : r + ROWS, :] = planes[p] * mask[p % 2, r : r + ROWS, :]
    own = [rim_velocity(m1[k], halo0[k], k) for k in range(4)]

    receive(3, lambda t: dg_recv.at[t], df_recv.at[0], df_recv.at[1])
    values = [dg_recv[t, i] for t in range(group) for i in (0, 1)] + [df_recv[0, 0], df_recv[1, 0]]
    fix3 = [rim_mask[k] * (own[k] + returned(values, k)) for k in range(4)]
    put_rims(fix3, 6, add_part)
    for r in blocks:
        columns = cols[6, r : r + ROWS, :]
        for p in range(8):
            sg_out[0, p // 2, p % 2, r : r + ROWS, :] = part[p, r : r + ROWS, :] + put_columns(columns, p)
    for copy in copies:
        copy.wait_send()


def shards(state, forcing, cotangent, neighbour, rotation, wet, levels):
    group = lax.axis_size("tile")
    hbm = pl.BlockSpec(memory_space=pltpu.HBM)
    vmem = pl.BlockSpec(memory_space=pltpu.VMEM)
    scalars = pl.BlockSpec(memory_space=pltpu.SMEM)
    fields, depth, side = state.shape[1], state.shape[2], state.shape[3]
    vm = lambda *shape: pltpu.VMEM(shape, F32)
    whole = lambda *shape: pltpu.VMEM(shape, jnp.int32)
    padded = vm(8, side + 2 * TOP, side)
    return pl.pallas_call(
        kernel,
        out_shape=(
            jax.ShapeDtypeStruct(state.shape, F32),
            jax.ShapeDtypeStruct(forcing.shape, F32),
        ),
        in_specs=[scalars] * 3 + [hbm] * 4,
        out_specs=(vmem, vmem),
        scratch_shapes=[
            vm(fields, depth, side, side), vm(fields, side, side), vm(fields, depth, side, side),
            whole(side, side), vm(depth, side, side),
            padded, padded, padded, padded,
            vm(8, side, side), vm(7, side, side),
            vm(4, 8, side), vm(group + 2, 4, 8, side),
            whole(8, side), whole(group + 2, 8, side),
            vm(4, 8, side), vm(3, 8, side), vm(3, 8, side), vm(group, 4, 8, side), vm(2, 3, 8, side),
            vm(2, 8, side), vm(1, 8, side), vm(1, 8, side), vm(group, 2, 8, side), vm(2, 1, 8, side),
            pltpu.SemaphoreType.DMA((4,)),
            pltpu.SemaphoreType.DMA((4, group + 1)), pltpu.SemaphoreType.DMA((4, group + 2)),
        ],
        compiler_params=pltpu.CompilerParams(
            collective_id=0, has_side_effects=True, vmem_limit_bytes=32 * 1024 * 1024
        ),
        name="window",
    )(neighbour, rotation, wet, *[pltpu.with_memory_space_constraint(x, pltpu.HBM) for x in (state, forcing, cotangent, levels)])


def solution(mesh):
    placed = (
        P(("face", "tile"), None, None, None, None),
        P(("face", "tile"), None, None, None, None),
        P(("face", "tile"), None, None, None, None),
        P(("face", "tile"), None),
        P(("face", "tile"), None),
        P(("face", "tile")),
        P(("face", "tile"), None, None),
    )
    return jax.shard_map(
        shards,
        mesh=mesh,
        in_specs=placed,
        out_specs=(
            P(("face", "tile"), None, None, None, None),
            P(("face", "tile"), None, None, None, None),
        ),
        check_vma=False,
    )
```
